512 devices in a mesh: pole: 4 (over x), prow: 8 (over y, core), pcol: 16 (over z).
Axes of the slice: x: 4, y: 4, z: 16, core: 2. Of those that a mesh axis runs over, the one named last changes fastest.
Arguments:
- anc_inverse: bfloat16 [32768, 8192], P(('pole', 'prow'), 'pcol'), parts along dimension 0, may hold values from -6 to 6
- factor_blocks: bfloat16 [64, 8, 256, 1024], P(('pole', 'pcol'), 'prow'), parts along dimension 0, may hold values from -0.125 to 0.125
- diag_in: float32 [64, 1024, 1024], P(('pole', 'pcol'), 'prow'), parts along dimension 0, may hold values from -6 to 6
- ancestors: int32 [16, 8], replicated, may hold values from 0 to 31, as said below
- active_count: int32 [16], replicated, may hold values from 6 to 8
Outputs:
- inverse_blocks: bfloat16 [64, 8, 256, 1024], P(('pole', 'pcol'), 'prow'), parts along dimension 0
- diagonal_inverse: float32 [64, 1024, 1024], P(('pole', 'pcol'), 'prow'), parts along dimension 0
The draws below stay inside these ranges and needn't reach their ends.
There are 4 independent parts, one for each index of `pole`. The reference program is written for one: setup_inputs(seed, part) draws one part's arguments, and reference() takes and returns one part's arrays. A program takes and returns all parts, laid end to end along the dimension named above; an argument that names none is the same for every part. Nothing has to cross between parts.
Inputs may be any that keep to these rules, and one draw needn't show every extreme that they name: ancestors[K, s] % 8 == s for every slot s, so the slots of one list name distinct ancestors with distinct values modulo 16.
All inputs are finite; a program needn't handle non-finite values.
Results may differ from the reference program's by a relative error of at most 0.013.
Values may be sent and summed in bfloat16 or wider, within the bound.
No kernel may reach another device: no remote copies, remote signals or barrier semaphores. Data moves between devices by JAX's collectives and lax.ppermute only.
A program may use at most 64 MiB of HBM per device.

```python
import jax
import jax.numpy as jnp
from jax import lax

ANC_W = 256
LEV_W = 1024
ANC_PER = 2
STRUCT = 8
ANC = 32
LEVEL_SN = 16
N_PROW = 8
N_PCOL = 16


def draw_ancestors(key, part):
    key = jax.random.fold_in(key, 11)
    first_key, second_key = jax.random.split(key)
    grid_cols = ANC // ANC_PER
    ratio = grid_cols // STRUCT
    upper = jax.random.randint(first_key, (LEVEL_SN, STRUCT), 0, ratio)
    layer = jax.random.randint(second_key, (LEVEL_SN, STRUCT), 0, ANC_PER)
    slots = jnp.arange(STRUCT, dtype=jnp.int32)[None, :]
    names = slots + STRUCT * upper + grid_cols * layer
    names = names.at[0, 0].set(0)
    names = names.at[0, STRUCT - 1].set(ANC - 1)
    return names.astype(jnp.int32)


def draw_active_count(key, part):
    key = jax.random.fold_in(key, 12)
    first_key, second_key, third_key = jax.random.split(key, 3)
    lowest = max(1, 3 * STRUCT // 4)
    counts = jax.random.randint(first_key, (LEVEL_SN,), lowest, STRUCT + 1)
    first_at = jax.random.randint(second_key, (), 0, LEVEL_SN)
    second_at = (first_at + 1 + jax.random.randint(third_key, (), 0, LEVEL_SN - 1)) % LEVEL_SN
    places = jnp.arange(LEVEL_SN, dtype=jnp.int32)
    counts = jnp.where(places == first_at, STRUCT, counts)
    counts = jnp.where(places == second_at, lowest, counts)
    return counts.astype(jnp.int32)


def steps_of(stream_key, extent, shards, smallest, largest):
    factor_of = 1.0
    for axis_at, shards_of in shards:
        heights = jax.random.uniform(jax.random.fold_in(jax.random.fold_in(stream_key, 6), axis_at), (shards_of,), jnp.float32, smallest / len(shards), largest / len(shards))
        factor_of = factor_of * jnp.repeat(jnp.exp(heights), extent[axis_at] // shards_of).reshape((-1,) + (1,) * (len(extent) - 1 - axis_at))
    return factor_of


def centred(own_key, dims, spread, limit, shards=(), held_as=jnp.bfloat16):
    values = jax.random.normal(own_key, dims, jnp.float32) * spread
    if len(shards) > 0:
        values = steps_of(own_key, dims, shards, -0.22, 0.18) * values
    return jnp.clip(values, min=-limit, max=limit).astype(held_as)


def setup_inputs(seed: int = 0, part: int = 0) -> dict:
    keys = jax.random.split(jax.random.key(seed), 6)
    own_keys = jax.random.split(jax.random.fold_in(keys[5], part), 6)
    return {
        "anc_inverse": centred(own_keys[0], (ANC * ANC_W, ANC * ANC_W), 1.0, 6.0, ((0, 8), (1, 16))),
        "factor_blocks": centred(own_keys[1], (LEVEL_SN, STRUCT, ANC_W, LEV_W), (STRUCT * ANC_W) ** -0.5, 0.125, ((0, 16), (1, 8))),
        "diag_in": centred(own_keys[2], (LEVEL_SN, LEV_W, LEV_W), 1.0, 6.0, ((0, 16), (1, 8)), jnp.float32),
        "ancestors": draw_ancestors(jax.random.fold_in(keys[5], 71), part),
        "active_count": draw_active_count(jax.random.fold_in(keys[5], 71), part),
    }


def reference(anc_inverse, factor_blocks, diag_in, ancestors, active_count):
    row_groups = ANC // N_PROW
    blocks = anc_inverse.reshape(ANC, ANC_W, ANC, ANC_W)

    def one_node(index):
        names = ancestors[index]
        row_pos = (names % N_PROW) * row_groups + names // N_PROW
        col_pos = (names % N_PCOL) * ANC_PER + names // N_PCOL
        chosen = blocks[row_pos][:, :, col_pos]
        live = (jnp.arange(STRUCT, dtype=jnp.int32) < active_count[index]).astype(jnp.float32)
        lower = factor_blocks[index].astype(jnp.float32) * live[:, None, None]
        product = -jnp.einsum("iajb,jbw->iaw", chosen.astype(jnp.float32), lower, precision=lax.Precision.HIGHEST)
        product = (product * live[:, None, None]).astype(jnp.bfloat16)
        diagonal = diag_in[index] - jnp.einsum("saw,sav->wv", lower, product.astype(jnp.float32), precision=lax.Precision.HIGHEST)
        return product, diagonal

    result = lax.map(one_node, jnp.arange(LEVEL_SN, dtype=jnp.int32))
    return (result[0], result[1])
```

```python
import functools

import jax
import jax.numpy as jnp
from jax import lax
from jax.experimental import pallas as pl
from jax.experimental.pallas import tpu as pltpu
from jax.sharding import PartitionSpec as P

W = 256
SLICE = 128
MIB = 1024 * 1024


def pick_kernel(rows, cols, anc_ref, a_ref, out_ref, sems):
    me_row = lax.axis_index("prow")
    me_col = lax.axis_index("pcol")
    slot = lax.rem(me_col, rows)
    copies = []
    for k in range(cols):
        i = anc_ref[k, me_row] // rows
        j = anc_ref[k, slot] // cols
        copy = pltpu.make_async_copy(
            a_ref.at[pl.ds(pl.multiple_of(i * W, W), W), pl.ds(pl.multiple_of(j * W, W), W)],
            out_ref.at[k],
            sems.at[k],
        )
        copy.start()
        copies.append(copy)
    for copy in copies:
        copy.wait()


def product_kernel(rows, cols, anc_ref, count_ref, a_ref, *refs):
    f_refs = refs[:rows]
    out_ref, held = refs[rows:]
    me_row = lax.axis_index("prow")
    me_col = lax.axis_index("pcol")
    count = count_ref[me_col]
    row_live = (me_row < count).astype(jnp.float32)
    for n in range(rows):
        t = slot_row(me_row, n, rows)
        live = (t < count).astype(jnp.bfloat16)
        held[n] = a_ref[lax.rem(anc_ref[me_col, t], cols)] * live
    width = out_ref.shape[-1]
    step = 256
    for at in range(0, width, step):
        total = jnp.zeros((W, step), jnp.float32)
        for n in range(rows):
            total += jnp.dot(held[n], f_refs[n][:, at : at + step], preferred_element_type=jnp.float32)
        out_ref[:, at : at + step] = (total * -row_live).astype(jnp.bfloat16)


def slot_row(me_row, n, rows):
    half = rows // 2
    base = me_row if n < half else me_row + 1 - 2 * lax.rem(me_row, 2)
    return lax.rem(base - 2 * (n % half) + rows, rows)


def turn_kernel(rows, own_ref, other_ref, out_ref):
    core = lax.rem(lax.axis_index("prow"), 2)
    for y in range(rows // 2):
        at = pl.ds(pl.multiple_of((2 * y + core) * SLICE, SLICE), SLICE)
        out_ref[pl.ds(y * SLICE, SLICE), 0:W] = own_ref[:, at].T
        out_ref[pl.ds(y * SLICE, SLICE), W : 2 * W] = other_ref[:, at].T


def term_kernel(turned_ref, own_ref, other_ref, out_ref):
    for y in range(out_ref.shape[0]):
        at = pl.ds(y * SLICE, SLICE)
        total = jnp.dot(turned_ref[at, 0:W], own_ref[...], preferred_element_type=jnp.float32)
        total += jnp.dot(turned_ref[at, W : 2 * W], other_ref[...], preferred_element_type=jnp.float32)
        out_ref[y] = total.astype(jnp.bfloat16)


def sum_kernel(diag_ref, terms_ref, out_ref):
    total = terms_ref[0].astype(jnp.float32)
    for y in range(1, terms_ref.shape[0]):
        total += terms_ref[y].astype(jnp.float32)
    out_ref[...] = diag_ref[...] - total


SMEM = pl.BlockSpec(memory_space=pltpu.SMEM)
VMEM = pl.BlockSpec(memory_space=pltpu.VMEM)
ANY = pl.BlockSpec(memory_space=pl.ANY)


def local(anc_inverse, factor_blocks, diag_in, ancestors, active_count):
    rows = lax.axis_size("prow")
    cols = lax.axis_size("pcol")
    chips = rows // 2
    width = factor_blocks.shape[-1]
    factor = factor_blocks[0, 0]

    def shift(x, h):
        return lax.ppermute(x, "prow", [(i, (i + 2 * h) % rows) for i in range(rows)])

    def swap(x):
        return lax.ppermute(x, "prow", [(i, i ^ 1) for i in range(rows)])

    sending = pl.pallas_call(
        functools.partial(pick_kernel, rows, cols),
        out_shape=jax.ShapeDtypeStruct((cols, W, W), jnp.bfloat16),
        in_specs=[SMEM, ANY],
        out_specs=ANY,
        scratch_shapes=[pltpu.SemaphoreType.DMA((cols,))],
        cost_estimate=pl.CostEstimate(flops=0, bytes_accessed=4 * MIB, transcendentals=0),
    )(ancestors, anc_inverse)
    arrived = lax.all_to_all(sending, "pcol", split_axis=0, concat_axis=0, tiled=True)

    same = [factor] + [shift(factor, h if h <= chips // 2 else h - chips) for h in range(1, chips)]
    factors = same + [swap(f) for f in same]
    turned = pl.pallas_call(
        functools.partial(turn_kernel, rows),
        out_shape=jax.ShapeDtypeStruct((chips * SLICE, 2 * W), jnp.bfloat16),
        in_specs=[VMEM, VMEM],
        out_specs=VMEM,
        compiler_params=pltpu.CompilerParams(vmem_limit_bytes=16 * MIB),
        cost_estimate=pl.CostEstimate(flops=0, bytes_accessed=2 * MIB, transcendentals=0),
    )(factors[0], factors[chips])

    product = pl.pallas_call(
        functools.partial(product_kernel, rows, cols),
        out_shape=jax.ShapeDtypeStruct((W, width), jnp.bfloat16),
        in_specs=[SMEM, SMEM] + [VMEM] * (1 + rows),
        out_specs=VMEM,
        scratch_shapes=[pltpu.VMEM((rows, W, W), jnp.bfloat16)],
        compiler_params=pltpu.CompilerParams(vmem_limit_bytes=32 * MIB),
        cost_estimate=pl.CostEstimate(flops=2 * rows * W * W * width, bytes_accessed=7 * MIB, transcendentals=0),
    )(ancestors, active_count, arrived, *factors)
    terms = pl.pallas_call(
        term_kernel,
        out_shape=jax.ShapeDtypeStruct((chips, SLICE, width), jnp.bfloat16),
        in_specs=[VMEM] * 3,
        out_specs=VMEM,
        compiler_params=pltpu.CompilerParams(vmem_limit_bytes=16 * MIB),
        cost_estimate=pl.CostEstimate(flops=4 * chips * SLICE * W * width, bytes_accessed=3 * MIB, transcendentals=0),
    )(turned, product, swap(product))
    groups = [list(range(core, rows, 2)) for core in range(2)]
    met = lax.all_to_all(terms, "prow", split_axis=0, concat_axis=0, tiled=True, axis_index_groups=groups)
    diagonal = pl.pallas_call(
        sum_kernel,
        out_shape=jax.ShapeDtypeStruct((SLICE, width), jnp.float32),
        in_specs=[VMEM, VMEM],
        out_specs=VMEM,
        compiler_params=pltpu.CompilerParams(vmem_limit_bytes=16 * MIB),
        cost_estimate=pl.CostEstimate(flops=0, bytes_accessed=2 * MIB, transcendentals=0),
    )(diag_in[0], met)
    return (product[None, None], diagonal[None])


def solution(mesh):
    placed = (
        P(("pole", "prow"), "pcol"),
        P(("pole", "pcol"), "prow", None, None),
        P(("pole", "pcol"), "prow", None),
        P(),
        P(),
    )
    return jax.shard_map(
        local,
        mesh=mesh,
        in_specs=placed,
        out_specs=(P(("pole", "pcol"), "prow", None, None), P(("pole", "pcol"), "prow", None)),
        check_vma=False,
    )
```

```python
import functools

import jax
import jax.numpy as jnp
from jax import lax
from jax.experimental import pallas as pl
from jax.experimental.pallas import tpu as pltpu
from jax.sharding import PartitionSpec as P

W = 256
SLICE = 128
MIB = 1024 * 1024


def pick_kernel(rows, cols, anc_ref, a_ref, out_ref, held, in_sems, out_sems):
    me_row = lax.axis_index("prow")
    me_col = lax.axis_index("pcol")
    slot = lax.rem(me_col, rows)
    high, wide = a_ref.shape[0] // W, a_ref.shape[1] // W
    loads = []
    for n in range(high * wide):
        i, j = n // wide, n % wide
        loads.append(
            pltpu.make_async_copy(a_ref.at[pl.ds(i * W, W), pl.ds(j * W, W)], held.at[n], in_sems.at[n])
        )
    for load in loads:
        load.start()
    picks = []
    for k in range(cols):
        picks.append((anc_ref[me_row, k] // rows) * wide + anc_ref[slot, k] // cols)
    for load in loads:
        load.wait()
    stores = [pltpu.make_async_copy(held.at[picks[k]], out_ref.at[k], out_sems.at[k]) for k in range(cols)]
    for store in stores:
        store.start()
    for store in stores:
        store.wait()


def product_kernel(rows, cols, anc_ref, count_ref, a_ref, *refs):
    f_refs = refs[:rows]
    out_ref, own_ref, held, factors, sems, out_sem = refs[rows:]
    loads = [pltpu.make_async_copy(f_refs[n], factors.at[n], sems.at[n]) for n in range(rows)]
    for load in loads:
        load.start()
    me_row = lax.axis_index("prow")
    me_col = lax.axis_index("pcol")
    count = count_ref[me_col]
    row_live = (me_row < count).astype(jnp.float32)
    for n in range(rows):
        t = slot_row(me_row, n, rows)
        live = (t < count).astype(jnp.bfloat16)
        held[n] = a_ref[lax.rem(anc_ref[t, me_col], cols)] * live
    for load in loads:
        load.wait()
    width = own_ref.shape[-1]
    step = 256
    for at in range(0, width, step):
        total = jnp.zeros((W, step), jnp.float32)
        for n in range(rows):
            total += jnp.dot(held[n], factors[n, :, at : at + step], preferred_element_type=jnp.float32)
        own_ref[:, at : at + step] = (total * -row_live).astype(jnp.bfloat16)
    store = pltpu.make_async_copy(own_ref, out_ref, out_sem)
    store.start()
    store.wait()


def slot_row(me_row, n, rows):
    half = rows // 2
    base = me_row if n < half else me_row + 1 - 2 * lax.rem(me_row, 2)
    return lax.rem(base - 2 * (n % half) + rows, rows)


def turn_kernel(rows, own_ref, other_ref, out_ref):
    core = lax.rem(lax.axis_index("prow"), 2)
    for y in range(rows // 2):
        at = pl.ds(pl.multiple_of((2 * y + core) * SLICE, SLICE), SLICE)
        out_ref[pl.ds(y * SLICE, SLICE), 0:W] = own_ref[:, at].T
        out_ref[pl.ds(y * SLICE, SLICE), W : 2 * W] = other_ref[:, at].T


def term_kernel(turned_ref, own_ref, other_ref, out_ref):
    for y in range(out_ref.shape[0]):
        at = pl.ds(y * SLICE, SLICE)
        total = jnp.dot(turned_ref[at, 0:W], own_ref[...], preferred_element_type=jnp.float32)
        total += jnp.dot(turned_ref[at, W : 2 * W], other_ref[...], preferred_element_type=jnp.float32)
        out_ref[y] = total.astype(jnp.bfloat16)


def sum_kernel(diag_ref, terms_ref, out_ref):
    total = terms_ref[0].astype(jnp.float32)
    for y in range(1, terms_ref.shape[0]):
        total += terms_ref[y].astype(jnp.float32)
    out_ref[...] = diag_ref[...] - total


SMEM = pl.BlockSpec(memory_space=pltpu.SMEM)
VMEM = pl.BlockSpec(memory_space=pltpu.VMEM)
HBM = pl.BlockSpec(memory_space=pltpu.HBM)


def local(anc_inverse, factor_blocks, diag_in, ancestors, active_count):
    rows = lax.axis_size("prow")
    cols = lax.axis_size("pcol")
    chips = rows // 2
    width = factor_blocks.shape[-1]
    factor = factor_blocks[0, 0]
    blocks = (anc_inverse.shape[0] // W) * (anc_inverse.shape[1] // W)
    lists = ancestors.T

    def shift(x, h):
        return lax.ppermute(x, "prow", [(i, (i + 2 * h) % rows) for i in range(rows)])

    def swap(x):
        return lax.ppermute(x, "prow", [(i, i ^ 1) for i in range(rows)])

    sending = pl.pallas_call(
        functools.partial(pick_kernel, rows, cols),
        out_shape=jax.ShapeDtypeStruct((cols, W, W), jnp.bfloat16),
        in_specs=[SMEM, HBM],
        out_specs=HBM,
        scratch_shapes=[
            pltpu.VMEM((blocks, W, W), jnp.bfloat16),
            pltpu.SemaphoreType.DMA((blocks,)),
            pltpu.SemaphoreType.DMA((cols,)),
        ],
        compiler_params=pltpu.CompilerParams(vmem_limit_bytes=16 * MIB),
        cost_estimate=pl.CostEstimate(flops=0, bytes_accessed=3 * MIB, transcendentals=0),
    )(lists, anc_inverse)
    arrived = lax.all_to_all(sending, "pcol", split_axis=0, concat_axis=0, tiled=True)

    same = [factor] + [shift(factor, h if h <= chips // 2 else h - chips) for h in range(1, chips)]
    factors = same + [swap(f) for f in same]
    turned = pl.pallas_call(
        functools.partial(turn_kernel, rows),
        out_shape=jax.ShapeDtypeStruct((chips * SLICE, 2 * W), jnp.bfloat16),
        in_specs=[VMEM, VMEM],
        out_specs=VMEM,
        compiler_params=pltpu.CompilerParams(vmem_limit_bytes=16 * MIB),
        cost_estimate=pl.CostEstimate(flops=0, bytes_accessed=2 * MIB, transcendentals=0),
    )(factors[0], factors[chips])

    product, own = pl.pallas_call(
        functools.partial(product_kernel, rows, cols),
        out_shape=(jax.ShapeDtypeStruct((W, width), jnp.bfloat16),) * 2,
        in_specs=[SMEM, SMEM, VMEM] + [HBM] * rows,
        out_specs=(HBM, VMEM),
        scratch_shapes=[
            pltpu.VMEM((rows, W, W), jnp.bfloat16),
            pltpu.VMEM((rows, W, width), jnp.bfloat16),
            pltpu.SemaphoreType.DMA((rows,)),
            pltpu.SemaphoreType.DMA,
        ],
        compiler_params=pltpu.CompilerParams(vmem_limit_bytes=32 * MIB),
        cost_estimate=pl.CostEstimate(flops=2 * rows * W * W * width, bytes_accessed=7 * MIB, transcendentals=0),
    )(lists, active_count, arrived, *factors)
    terms = pl.pallas_call(
        term_kernel,
        out_shape=jax.ShapeDtypeStruct((chips, SLICE, width), jnp.bfloat16),
        in_specs=[VMEM] * 3,
        out_specs=VMEM,
        compiler_params=pltpu.CompilerParams(vmem_limit_bytes=16 * MIB),
        cost_estimate=pl.CostEstimate(flops=4 * chips * SLICE * W * width, bytes_accessed=3 * MIB, transcendentals=0),
    )(turned, own, swap(own))
    groups = [list(range(core, rows, 2)) for core in range(2)]
    met = lax.all_to_all(terms, "prow", split_axis=0, concat_axis=0, tiled=True, axis_index_groups=groups)
    diagonal = pl.pallas_call(
        sum_kernel,
        out_shape=jax.ShapeDtypeStruct((SLICE, width), jnp.float32),
        in_specs=[VMEM, VMEM],
        out_specs=VMEM,
        compiler_params=pltpu.CompilerParams(vmem_limit_bytes=16 * MIB),
        cost_estimate=pl.CostEstimate(flops=0, bytes_accessed=2 * MIB, transcendentals=0),
    )(diag_in[0], met)
    return (product[None, None], diagonal[None])


def solution(mesh):
    placed = (
        P(("pole", "prow"), "pcol"),
        P(("pole", "pcol"), "prow", None, None),
        P(("pole", "pcol"), "prow", None),
        P(),
        P(),
    )
    return jax.shard_map(
        local,
        mesh=mesh,
        in_specs=placed,
        out_specs=(P(("pole", "pcol"), "prow", None, None), P(("pole", "pcol"), "prow", None)),
        check_vma=False,
    )
```

```python
import functools

import jax
import jax.numpy as jnp
from jax import lax
from jax.experimental import pallas as pl
from jax.experimental.pallas import tpu as pltpu
from jax.sharding import PartitionSpec as P

W = 256
SLICE = 128
MIB = 1024 * 1024


def pick_kernel(rows, cols, anc_ref, a_ref, out_ref, held, in_sems, out_sems):
    high, wide = a_ref.shape[0] // W, a_ref.shape[1] // W
    loads = []
    for n in range(high * wide):
        i, j = n // wide, n % wide
        load = pltpu.make_async_copy(a_ref.at[pl.ds(i * W, W), pl.ds(j * W, W)], held.at[n], in_sems.at[n])
        load.start()
        loads.append(load)
    me_row = lax.axis_index("prow")
    me_col = lax.axis_index("pcol")
    slot = lax.rem(me_col, rows)
    stores = []
    for k in range(cols):
        name = anc_ref[slot, k]
        pick = (anc_ref[me_row, k] // rows) * wide + name // cols
        store = pltpu.make_async_copy(held.at[pick], out_ref.at[k], out_sems.at[k])
        stores.append((lax.rem(name, cols) == me_col, store))
    for load in loads:
        load.wait()
    for owed, store in stores:
        pl.when(owed)(store.start)
    for owed, store in stores:
        pl.when(owed)(store.wait)


def product_kernel(rows, cols, anc_ref, count_ref, a_ref, f_ref, out_ref, own_ref, held, factors, total, sems, out_sems):
    half = rows // 2
    width = own_ref.shape[-1]
    step = 256
    loads = []
    for n in range(rows):
        load = pltpu.make_async_copy(f_ref.at[n], factors.at[n], sems.at[n])
        load.start()
        loads.append(load)
    me_row = lax.axis_index("prow")
    me_col = lax.axis_index("pcol")
    count = count_ref[me_col]
    row_live = (me_row < count).astype(jnp.float32)
    for n in range(rows):
        t = slot_row(me_row, n, rows)
        live = (t < count).astype(jnp.bfloat16)
        held[n] = a_ref[lax.rem(anc_ref[t, me_col], cols)] * live
    stores = []
    for n in range(0, rows, 2):
        loads[n].wait()
        loads[n + 1].wait()
        for q in range(width // step):
            at = pl.ds(q * step, step)
            part = jnp.dot(held[n], factors[n, :, at], preferred_element_type=jnp.float32)
            part += jnp.dot(held[n + 1], factors[n + 1, :, at], preferred_element_type=jnp.float32)
            if n > 0:
                part += total[:, at]
            if n < rows - 2:
                total[:, at] = part
            else:
                own_ref[:, at] = (part * -row_live).astype(jnp.bfloat16)
                store = pltpu.make_async_copy(own_ref.at[:, at], out_ref.at[:, at], out_sems.at[q])
                store.start()
                stores.append(store)
    for store in stores:
        store.wait()


def slot_row(me_row, n, rows):
    half = rows // 2
    base = me_row if n < half else me_row + 1 - 2 * lax.rem(me_row, 2)
    return lax.rem(base - 2 * (n % half) + rows, rows)


def turn_kernel(rows, f_ref, out_ref, held, sems):
    half = rows // 2
    loads = [pltpu.make_async_copy(f_ref.at[n * half], held.at[n], sems.at[n]) for n in range(2)]
    for load in loads:
        load.start()
    for load in loads:
        load.wait()
    core = lax.rem(lax.axis_index("prow"), 2)
    for y in range(half):
        at = pl.ds(pl.multiple_of((2 * y + core) * SLICE, SLICE), SLICE)
        for n in range(2):
            out_ref[pl.ds(y * SLICE, SLICE), n * W : (n + 1) * W] = held[n, :, at].T


def term_kernel(turned_ref, own_ref, other_ref, out_ref):
    for y in range(out_ref.shape[0]):
        at = pl.ds(y * SLICE, SLICE)
        total = jnp.dot(turned_ref[at, 0:W], own_ref[...], preferred_element_type=jnp.float32)
        total += jnp.dot(turned_ref[at, W : 2 * W], other_ref[...], preferred_element_type=jnp.float32)
        out_ref[y] = total.astype(jnp.bfloat16)


def sum_kernel(diag_ref, terms_ref, out_ref):
    total = terms_ref[0].astype(jnp.float32)
    for y in range(1, terms_ref.shape[0]):
        total += terms_ref[y].astype(jnp.float32)
    out_ref[...] = diag_ref[...] - total


SMEM = pl.BlockSpec(memory_space=pltpu.SMEM)
VMEM = pl.BlockSpec(memory_space=pltpu.VMEM)
HBM = pl.BlockSpec(memory_space=pltpu.HBM)


def local(anc_inverse, factor_blocks, diag_in, ancestors, active_count):
    rows = lax.axis_size("prow")
    cols = lax.axis_size("pcol")
    chips = rows // 2
    width = factor_blocks.shape[-1]
    factor = factor_blocks[0, 0]
    lists = ancestors.T

    def shift(x, h):
        return lax.ppermute(x, "prow", [(i, (i + 2 * h) % rows) for i in range(rows)])

    def swap(x):
        return lax.ppermute(x, "prow", [(i, i ^ 1) for i in range(rows)])

    blocks = (anc_inverse.shape[0] // W) * (anc_inverse.shape[1] // W)
    sending = pl.pallas_call(
        functools.partial(pick_kernel, rows, cols),
        out_shape=jax.ShapeDtypeStruct((cols, W, W), jnp.bfloat16),
        in_specs=[SMEM, HBM],
        out_specs=HBM,
        scratch_shapes=[
            pltpu.VMEM((blocks, W, W), jnp.bfloat16),
            pltpu.SemaphoreType.DMA((blocks,)),
            pltpu.SemaphoreType.DMA((cols,)),
        ],
        compiler_params=pltpu.CompilerParams(vmem_limit_bytes=60 * MIB),
        cost_estimate=pl.CostEstimate(flops=0, bytes_accessed=3 * MIB, transcendentals=0),
    )(lists, anc_inverse)
    arrived = lax.all_to_all(sending, "pcol", split_axis=0, concat_axis=0, tiled=True)

    same = jnp.stack([factor] + [shift(factor, h if h <= chips // 2 else h - chips) for h in range(1, chips)])
    factors = jnp.concatenate([same, swap(same)])
    turned = pl.pallas_call(
        functools.partial(turn_kernel, rows),
        out_shape=jax.ShapeDtypeStruct((chips * SLICE, 2 * W), jnp.bfloat16),
        in_specs=[HBM],
        out_specs=VMEM,
        scratch_shapes=[pltpu.VMEM((2, W, width), jnp.bfloat16), pltpu.SemaphoreType.DMA((2,))],
        compiler_params=pltpu.CompilerParams(vmem_limit_bytes=50 * MIB),
        cost_estimate=pl.CostEstimate(flops=0, bytes_accessed=2 * MIB, transcendentals=0),
    )(factors)
    arrived, turned = lax.optimization_barrier((arrived, turned))

    product, own = pl.pallas_call(
        functools.partial(product_kernel, rows, cols),
        out_shape=(jax.ShapeDtypeStruct((W, width), jnp.bfloat16),) * 2,
        in_specs=[SMEM, SMEM, VMEM, HBM],
        out_specs=(HBM, VMEM),
        scratch_shapes=[
            pltpu.VMEM((rows, W, W), jnp.bfloat16),
            pltpu.VMEM((rows, W, width), jnp.bfloat16),
            pltpu.VMEM((W, width), jnp.float32),
            pltpu.SemaphoreType.DMA((rows,)),
            pltpu.SemaphoreType.DMA((width // 256,)),
        ],
        compiler_params=pltpu.CompilerParams(vmem_limit_bytes=50 * MIB),
        cost_estimate=pl.CostEstimate(flops=2 * rows * W * W * width, bytes_accessed=7 * MIB, transcendentals=0),
    )(lists, active_count, arrived, factors)
    terms = pl.pallas_call(
        term_kernel,
        out_shape=jax.ShapeDtypeStruct((chips, SLICE, width), jnp.bfloat16),
        in_specs=[VMEM] * 3,
        out_specs=VMEM,
        compiler_params=pltpu.CompilerParams(vmem_limit_bytes=16 * MIB),
        cost_estimate=pl.CostEstimate(flops=4 * chips * SLICE * W * width, bytes_accessed=3 * MIB, transcendentals=0),
    )(turned, own, swap(own))
    groups = [list(range(core, rows, 2)) for core in range(2)]
    met = lax.all_to_all(terms, "prow", split_axis=0, concat_axis=0, tiled=True, axis_index_groups=groups)
    diagonal = pl.pallas_call(
        sum_kernel,
        out_shape=jax.ShapeDtypeStruct((SLICE, width), jnp.float32),
        in_specs=[VMEM, VMEM],
        out_specs=VMEM,
        compiler_params=pltpu.CompilerParams(vmem_limit_bytes=16 * MIB),
        cost_estimate=pl.CostEstimate(flops=0, bytes_accessed=2 * MIB, transcendentals=0),
    )(diag_in[0], met)
    return (product[None, None], diagonal[None])


def solution(mesh):
    placed = (
        P(("pole", "prow"), "pcol"),
        P(("pole", "pcol"), "prow", None, None),
        P(("pole", "pcol"), "prow", None),
        P(),
        P(),
    )
    return jax.shard_map(
        local,
        mesh=mesh,
        in_specs=placed,
        out_specs=(P(("pole", "pcol"), "prow", None, None), P(("pole", "pcol"), "prow", None)),
        check_vma=False,
    )
```

```python
import functools

import jax
import jax.numpy as jnp
from jax import lax
from jax.experimental import pallas as pl
from jax.experimental.pallas import tpu as pltpu
from jax.sharding import PartitionSpec as P

W = 256
SLICE = 128
MIB = 1024 * 1024


def pick_kernel(rows, cols, anc_ref, a_ref, out_ref, names, held, names_sem, in_sems, out_sems):
    high, wide = a_ref.shape[0] // W, a_ref.shape[1] // W
    part = W // 2
    fetch = pltpu.make_async_copy(anc_ref, names, names_sem)
    fetch.start()
    loads = []
    for p in range(2):
        for n in range(high * wide):
            i, j = n // wide, n % wide
            load = pltpu.make_async_copy(
                a_ref.at[pl.ds(i * W + p * part, part), pl.ds(j * W, W)],
                held.at[n, pl.ds(p * part, part)],
                in_sems.at[p, n],
            )
            load.start()
            loads.append(load)
    me_row = lax.axis_index("prow")
    me_col = lax.axis_index("pcol")
    slot = lax.rem(me_col, rows)
    fetch.wait()
    owed, picks = [], []
    for k in range(cols):
        name = names[slot, k]
        picks.append((names[me_row, k] // rows) * wide + name // cols)
        owed.append(lax.rem(name, cols) == me_col)
    stores = []
    for p in range(2):
        for load in loads[p * high * wide : (p + 1) * high * wide]:
            load.wait()
        at = pl.ds(p * part, part)
        for k in range(cols):
            store = pltpu.make_async_copy(held.at[picks[k], at], out_ref.at[k, at], out_sems.at[p, k])
            pl.when(owed[k])(store.start)
            stores.append((owed[k], store))
    for needed, store in stores:
        pl.when(needed)(store.wait)


def product_kernel(rows, cols, anc_ref, count_ref, a_ref, f_ref, out_ref, own_ref, held, factors, total, sems, out_sems):
    half = rows // 2
    width = own_ref.shape[-1]
    step = 256
    loads = []
    for n in range(rows):
        load = pltpu.make_async_copy(f_ref.at[n], factors.at[n], sems.at[n])
        load.start()
        loads.append(load)
    me_row = lax.axis_index("prow")
    me_col = lax.axis_index("pcol")
    count = count_ref[me_col]
    row_live = (me_row < count).astype(jnp.float32)
    for n in range(rows):
        t = slot_row(me_row, n, rows)
        live = (t < count).astype(jnp.bfloat16)
        held[n] = a_ref[lax.rem(anc_ref[t, me_col], cols)] * live
    stores = []
    for n in range(0, rows, 2):
        for load in loads[n : n + 2]:
            load.wait()
        for q in range(width // step):
            at = pl.ds(q * step, step)
            part = jnp.dot(held[n], factors[n, :, at], preferred_element_type=jnp.float32)
            part += jnp.dot(held[n + 1], factors[n + 1, :, at], preferred_element_type=jnp.float32)
            if n > 0:
                part += total[:, at]
            if n < rows - 2:
                total[:, at] = part
            else:
                own_ref[:, at] = (part * -row_live).astype(jnp.bfloat16)
                store = pltpu.make_async_copy(own_ref.at[:, at], out_ref.at[:, at], out_sems.at[q])
                store.start()
                stores.append(store)
    for store in stores:
        store.wait()


def slot_row(me_row, n, rows):
    half = rows // 2
    base = me_row if n < half else me_row + 1 - 2 * lax.rem(me_row, 2)
    return lax.rem(base - 2 * (n % half) + rows, rows)


def turn_kernel(rows, f_ref, out_ref, held, sems):
    half = rows // 2
    loads = [pltpu.make_async_copy(f_ref.at[n * half], held.at[n], sems.at[n]) for n in range(2)]
    for load in loads:
        load.start()
    for load in loads:
        load.wait()
    me = lax.axis_index("prow")
    y, core = me // 2, lax.rem(me, 2)
    for p, h in enumerate((2, 1, 3, 0)):
        at = pl.ds(pl.multiple_of((2 * lax.rem(y + h, half) + core) * SLICE, SLICE), SLICE)
        for n in range(2):
            out_ref[pl.ds(p * SLICE, SLICE), n * W : (n + 1) * W] = held[n, :, at].T


def term_kernel(base, turned_ref, own_ref, other_ref, *out_refs):
    for n, ref in enumerate(out_refs):
        at = pl.ds((base + n) * SLICE, SLICE)
        total = jnp.dot(turned_ref[at, 0:W], own_ref[...], preferred_element_type=jnp.float32)
        total += jnp.dot(turned_ref[at, W : 2 * W], other_ref[...], preferred_element_type=jnp.float32)
        ref[...] = total.astype(ref.dtype)


def sum_kernel(diag_ref, kept_ref, *refs):
    total = kept_ref[...]
    for ref in refs[:-1]:
        total += ref[...].astype(jnp.float32)
    refs[-1][...] = diag_ref[...] - total


SMEM = pl.BlockSpec(memory_space=pltpu.SMEM)
VMEM = pl.BlockSpec(memory_space=pltpu.VMEM)
HBM = pl.BlockSpec(memory_space=pltpu.HBM)


def local(anc_inverse, factor_blocks, diag_in, ancestors, active_count):
    rows = lax.axis_size("prow")
    cols = lax.axis_size("pcol")
    chips = rows // 2
    width = factor_blocks.shape[-1]
    factor = factor_blocks[0, 0]
    lists = ancestors.T

    def shift(x, h):
        return lax.ppermute(x, "prow", [(i, (i + 2 * h) % rows) for i in range(rows)])

    def swap(x):
        return lax.ppermute(x, "prow", [(i, i ^ 1) for i in range(rows)])

    blocks = (anc_inverse.shape[0] // W) * (anc_inverse.shape[1] // W)
    sending = pl.pallas_call(
        functools.partial(pick_kernel, rows, cols),
        out_shape=jax.ShapeDtypeStruct((cols, W, W), jnp.bfloat16),
        in_specs=[HBM, HBM],
        out_specs=HBM,
        scratch_shapes=[
            pltpu.SMEM((rows, cols), jnp.int32),
            pltpu.VMEM((blocks, W, W), jnp.bfloat16),
            pltpu.SemaphoreType.DMA,
            pltpu.SemaphoreType.DMA((2, blocks)),
            pltpu.SemaphoreType.DMA((2, cols)),
        ],
        compiler_params=pltpu.CompilerParams(vmem_limit_bytes=60 * MIB),
        cost_estimate=pl.CostEstimate(flops=0, bytes_accessed=3 * MIB, transcendentals=0),
    )(lists, anc_inverse)
    arrived = lax.all_to_all(sending, "pcol", split_axis=0, concat_axis=0, tiled=True)

    same = jnp.stack([factor] + [shift(factor, h if h <= chips // 2 else h - chips) for h in range(1, chips)])
    factors = jnp.concatenate([same, swap(same)])
    turned = pl.pallas_call(
        functools.partial(turn_kernel, rows),
        out_shape=jax.ShapeDtypeStruct((chips * SLICE, 2 * W), jnp.bfloat16),
        in_specs=[HBM],
        out_specs=VMEM,
        scratch_shapes=[pltpu.VMEM((2, W, width), jnp.bfloat16), pltpu.SemaphoreType.DMA((2,))],
        compiler_params=pltpu.CompilerParams(vmem_limit_bytes=50 * MIB),
        cost_estimate=pl.CostEstimate(flops=0, bytes_accessed=2 * MIB, transcendentals=0),
    )(factors)
    arrived, turned = lax.optimization_barrier((arrived, turned))

    product, own = pl.pallas_call(
        functools.partial(product_kernel, rows, cols),
        out_shape=(jax.ShapeDtypeStruct((W, width), jnp.bfloat16),) * 2,
        in_specs=[SMEM, SMEM, VMEM, HBM],
        out_specs=(HBM, VMEM),
        scratch_shapes=[
            pltpu.VMEM((rows, W, W), jnp.bfloat16),
            pltpu.VMEM((rows, W, width), jnp.bfloat16),
            pltpu.VMEM((W, width), jnp.float32),
            pltpu.SemaphoreType.DMA((rows,)),
            pltpu.SemaphoreType.DMA((width // 256,)),
        ],
        compiler_params=pltpu.CompilerParams(vmem_limit_bytes=50 * MIB),
        cost_estimate=pl.CostEstimate(flops=2 * rows * W * W * width, bytes_accessed=7 * MIB, transcendentals=0),
    )(lists, active_count, arrived, factors)
    other = swap(own)

    def terms(base, dtypes):
        return pl.pallas_call(
            functools.partial(term_kernel, base),
            out_shape=[jax.ShapeDtypeStruct((SLICE, width), dtype) for dtype in dtypes],
            in_specs=[VMEM] * 3,
            out_specs=[VMEM] * len(dtypes),
            compiler_params=pltpu.CompilerParams(vmem_limit_bytes=16 * MIB),
            cost_estimate=pl.CostEstimate(flops=4 * len(dtypes) * SLICE * W * width, bytes_accessed=2 * MIB, transcendentals=0),
        )(turned, own, other)

    (far,) = terms(0, [jnp.bfloat16])
    met = [shift(far, 2)]
    near, back, kept = terms(1, [jnp.bfloat16, jnp.bfloat16, jnp.float32])
    met += [shift(near, 1), shift(back, -1)]
    diagonal = pl.pallas_call(
        sum_kernel,
        out_shape=jax.ShapeDtypeStruct((SLICE, width), jnp.float32),
        in_specs=[VMEM] * (chips + 1),
        out_specs=VMEM,
        compiler_params=pltpu.CompilerParams(vmem_limit_bytes=16 * MIB),
        cost_estimate=pl.CostEstimate(flops=0, bytes_accessed=2 * MIB, transcendentals=0),
    )(diag_in[0], kept, *met)
    return (product[None, None], diagonal[None])


def solution(mesh):
    placed = (
        P(("pole", "prow"), "pcol"),
        P(("pole", "pcol"), "prow", None, None),
        P(("pole", "pcol"), "prow", None),
        P(),
        P(),
    )
    return jax.shard_map(
        local,
        mesh=mesh,
        in_specs=placed,
        out_specs=(P(("pole", "pcol"), "prow", None, None), P(("pole", "pcol"), "prow", None)),
        check_vma=False,
    )
```

```python
import functools

import jax
import jax.numpy as jnp
from jax import lax
from jax.experimental import pallas as pl
from jax.experimental.pallas import tpu as pltpu
from jax.sharding import PartitionSpec as P

W = 256
SLICE = 128
MIB = 1024 * 1024


def pick_kernel(rows, cols, anc_ref, a_ref, out_ref, names, held, names_sem, in_sems, out_sems):
    high, wide = a_ref.shape[0] // W, a_ref.shape[1] // W
    part = W // 2
    fetch = pltpu.make_async_copy(anc_ref, names, names_sem)
    fetch.start()
    loads = []
    for p in range(2):
        for n in range(high * wide):
            i, j = n // wide, n % wide
            load = pltpu.make_async_copy(
                a_ref.at[pl.ds(i * W + p * part, part), pl.ds(j * W, W)],
                held.at[n, pl.ds(p * part, part)],
                in_sems.at[p, n],
            )
            load.start()
            loads.append(load)
    me_row = lax.axis_index("prow")
    me_col = lax.axis_index("pcol")
    slot = lax.rem(me_col, rows)
    fetch.wait()
    owed, picks = [], []
    for k in range(cols):
        name = names[slot, k]
        picks.append((names[me_row, k] // rows) * wide + name // cols)
        owed.append(lax.rem(name, cols) == me_col)
    stores = []
    for p in range(2):
        for load in loads[p * high * wide : (p + 1) * high * wide]:
            load.wait()
        at = pl.ds(p * part, part)
        for k in range(cols):
            store = pltpu.make_async_copy(held.at[picks[k], at], out_ref.at[k, at], out_sems.at[p, k])
            pl.when(owed[k])(store.start)
            stores.append((owed[k], store))
    for needed, store in stores:
        pl.when(needed)(store.wait)


def product_kernel(rows, cols, anc_ref, count_ref, a_ref, f_ref, own_ref, held, factors, total, sems):
    half = rows // 2
    width = own_ref.shape[-1]
    step = 256
    loads = []
    for n in range(rows):
        load = pltpu.make_async_copy(f_ref.at[n], factors.at[n], sems.at[n])
        load.start()
        loads.append(load)
    me_row = lax.axis_index("prow")
    me_col = lax.axis_index("pcol")
    count = count_ref[me_col]
    row_live = (me_row < count).astype(jnp.float32)
    for n in range(rows):
        t = slot_row(me_row, n, rows)
        live = (t < count).astype(jnp.bfloat16)
        held[n] = a_ref[lax.rem(anc_ref[t, me_col], cols)] * live
    for n in range(0, rows, 2):
        for load in loads[n : n + 2]:
            load.wait()
        for q in range(width // step):
            at = pl.ds(q * step, step)
            part = jnp.dot(held[n], factors[n, :, at], preferred_element_type=jnp.float32)
            part += jnp.dot(held[n + 1], factors[n + 1, :, at], preferred_element_type=jnp.float32)
            if n > 0:
                part += total[:, at]
            if n < rows - 2:
                total[:, at] = part
            else:
                own_ref[:, at] = (part * -row_live).astype(jnp.bfloat16)


def slot_row(me_row, n, rows):
    half = rows // 2
    base = me_row if n < half else me_row + 1 - 2 * lax.rem(me_row, 2)
    return lax.rem(base - 2 * (n % half) + rows, rows)


def turn_kernel(rows, f_ref, out_ref, held, sems):
    half = rows // 2
    loads = [pltpu.make_async_copy(f_ref.at[n * half], held.at[n], sems.at[n]) for n in range(2)]
    for load in loads:
        load.start()
    for load in loads:
        load.wait()
    me = lax.axis_index("prow")
    y, core = me // 2, lax.rem(me, 2)
    for p, h in enumerate((2, 1, 3, 0)):
        at = pl.ds(pl.multiple_of((2 * lax.rem(y + h, half) + core) * SLICE, SLICE), SLICE)
        for n in range(2):
            out_ref[pl.ds(p * SLICE, SLICE), n * W : (n + 1) * W] = held[n, :, at].T


def term_kernel(base, turned_ref, own_ref, other_ref, *out_refs):
    for n, ref in enumerate(out_refs):
        at = pl.ds((base + n) * SLICE, SLICE)
        total = jnp.dot(turned_ref[at, 0:W], own_ref[...], preferred_element_type=jnp.float32)
        total += jnp.dot(turned_ref[at, W : 2 * W], other_ref[...], preferred_element_type=jnp.float32)
        ref[...] = total.astype(ref.dtype)


def store_kernel(own_ref, out_ref, sem):
    store = pltpu.make_async_copy(own_ref, out_ref, sem)
    store.start()
    store.wait()


def sum_kernel(diag_ref, kept_ref, *refs):
    total = kept_ref[...]
    for ref in refs[:-1]:
        total += ref[...].astype(jnp.float32)
    refs[-1][...] = diag_ref[...] - total


SMEM = pl.BlockSpec(memory_space=pltpu.SMEM)
VMEM = pl.BlockSpec(memory_space=pltpu.VMEM)
HBM = pl.BlockSpec(memory_space=pltpu.HBM)


def local(anc_inverse, factor_blocks, diag_in, ancestors, active_count):
    rows = lax.axis_size("prow")
    cols = lax.axis_size("pcol")
    chips = rows // 2
    width = factor_blocks.shape[-1]
    factor = factor_blocks[0, 0]
    lists = ancestors.T

    def shift(x, h):
        return lax.ppermute(x, "prow", [(i, (i + 2 * h) % rows) for i in range(rows)])

    def swap(x):
        return lax.ppermute(x, "prow", [(i, i ^ 1) for i in range(rows)])

    blocks = (anc_inverse.shape[0] // W) * (anc_inverse.shape[1] // W)
    sending = pl.pallas_call(
        functools.partial(pick_kernel, rows, cols),
        out_shape=jax.ShapeDtypeStruct((cols, W, W), jnp.bfloat16),
        in_specs=[HBM, HBM],
        out_specs=HBM,
        scratch_shapes=[
            pltpu.SMEM((rows, cols), jnp.int32),
            pltpu.VMEM((blocks, W, W), jnp.bfloat16),
            pltpu.SemaphoreType.DMA,
            pltpu.SemaphoreType.DMA((2, blocks)),
            pltpu.SemaphoreType.DMA((2, cols)),
        ],
        compiler_params=pltpu.CompilerParams(vmem_limit_bytes=60 * MIB),
        cost_estimate=pl.CostEstimate(flops=0, bytes_accessed=3 * MIB, transcendentals=0),
    )(lists, anc_inverse)
    arrived = lax.all_to_all(sending, "pcol", split_axis=0, concat_axis=0, tiled=True)

    same = jnp.stack([factor] + [shift(factor, h if h <= chips // 2 else h - chips) for h in range(1, chips)])
    factors = jnp.concatenate([same, swap(same)])
    turned = pl.pallas_call(
        functools.partial(turn_kernel, rows),
        out_shape=jax.ShapeDtypeStruct((chips * SLICE, 2 * W), jnp.bfloat16),
        in_specs=[HBM],
        out_specs=VMEM,
        scratch_shapes=[pltpu.VMEM((2, W, width), jnp.bfloat16), pltpu.SemaphoreType.DMA((2,))],
        compiler_params=pltpu.CompilerParams(vmem_limit_bytes=50 * MIB),
        cost_estimate=pl.CostEstimate(flops=0, bytes_accessed=2 * MIB, transcendentals=0),
    )(factors)
    arrived, turned = lax.optimization_barrier((arrived, turned))

    own = pl.pallas_call(
        functools.partial(product_kernel, rows, cols),
        out_shape=jax.ShapeDtypeStruct((W, width), jnp.bfloat16),
        in_specs=[SMEM, SMEM, VMEM, HBM],
        out_specs=VMEM,
        scratch_shapes=[
            pltpu.VMEM((rows, W, W), jnp.bfloat16),
            pltpu.VMEM((rows, W, width), jnp.bfloat16),
            pltpu.VMEM((W, width), jnp.float32),
            pltpu.SemaphoreType.DMA((rows,)),
        ],
        compiler_params=pltpu.CompilerParams(vmem_limit_bytes=50 * MIB),
        cost_estimate=pl.CostEstimate(flops=2 * rows * W * W * width, bytes_accessed=7 * MIB, transcendentals=0),
    )(lists, active_count, arrived, factors)
    other = swap(own)

    def terms(base, dtypes):
        return pl.pallas_call(
            functools.partial(term_kernel, base),
            out_shape=[jax.ShapeDtypeStruct((SLICE, width), dtype) for dtype in dtypes],
            in_specs=[VMEM] * 3,
            out_specs=[VMEM] * len(dtypes),
            compiler_params=pltpu.CompilerParams(vmem_limit_bytes=16 * MIB),
            cost_estimate=pl.CostEstimate(flops=4 * len(dtypes) * SLICE * W * width, bytes_accessed=2 * MIB, transcendentals=0),
        )(turned, own, other)

    (far,) = terms(0, [jnp.bfloat16])
    met = [shift(far, 2)]
    near, back, kept = terms(1, [jnp.bfloat16, jnp.bfloat16, jnp.float32])
    met += [shift(near, 1), shift(back, -1)]
    product = pl.pallas_call(
        store_kernel,
        out_shape=jax.ShapeDtypeStruct((W, width), jnp.bfloat16),
        in_specs=[VMEM],
        out_specs=HBM,
        scratch_shapes=[pltpu.SemaphoreType.DMA],
        compiler_params=pltpu.CompilerParams(vmem_limit_bytes=16 * MIB),
        cost_estimate=pl.CostEstimate(flops=0, bytes_accessed=MIB, transcendentals=0),
    )(own)
    diagonal = pl.pallas_call(
        sum_kernel,
        out_shape=jax.ShapeDtypeStruct((SLICE, width), jnp.float32),
        in_specs=[VMEM] * (chips + 1),
        out_specs=VMEM,
        compiler_params=pltpu.CompilerParams(vmem_limit_bytes=16 * MIB),
        cost_estimate=pl.CostEstimate(flops=0, bytes_accessed=2 * MIB, transcendentals=0),
    )(diag_in[0], kept, *met)
    return (product[None, None], diagonal[None])


def solution(mesh):
    placed = (
        P(("pole", "prow"), "pcol"),
        P(("pole", "pcol"), "prow", None, None),
        P(("pole", "pcol"), "prow", None),
        P(),
        P(),
    )
    return jax.shard_map(
        local,
        mesh=mesh,
        in_specs=placed,
        out_specs=(P(("pole", "pcol"), "prow", None, None), P(("pole", "pcol"), "prow", None)),
        check_vma=False,
    )
```

```python
import functools

import jax
import jax.numpy as jnp
from jax import lax
from jax.experimental import pallas as pl
from jax.experimental.pallas import tpu as pltpu
from jax.sharding import PartitionSpec as P

W = 256
SLICE = 128
MIB = 1024 * 1024


def pick_kernel(rows, cols, anc_ref, a_ref, out_ref, names, held, names_sem, in_sems, out_sems):
    high, wide = a_ref.shape[0] // W, a_ref.shape[1] // W
    part = W // 2
    fetch = pltpu.make_async_copy(anc_ref, names, names_sem)
    fetch.start()
    loads = []
    for p in range(2):
        for n in range(high * wide):
            i, j = n // wide, n % wide
            load = pltpu.make_async_copy(
                a_ref.at[pl.ds(i * W + p * part, part), pl.ds(j * W, W)],
                held.at[n, pl.ds(p * part, part)],
                in_sems.at[p, n],
            )
            load.start()
            loads.append(load)
    me_row = lax.axis_index("prow")
    me_col = lax.axis_index("pcol")
    slot = lax.rem(me_col, rows)
    fetch.wait()
    owed, picks = [], []
    for k in range(cols):
        name = names[slot, k]
        picks.append((names[me_row, k] // rows) * wide + name // cols)
        owed.append(lax.rem(name, cols) == me_col)
    stores = []
    for p in range(2):
        for load in loads[p * high * wide : (p + 1) * high * wide]:
            load.wait()
        at = pl.ds(p * part, part)
        for k in range(cols):
            store = pltpu.make_async_copy(held.at[picks[k], at], out_ref.at[k, at], out_sems.at[p, k])
            pl.when(owed[k])(store.start)
            stores.append((owed[k], store))
    for needed, store in stores:
        pl.when(needed)(store.wait)


def product_kernel(rows, cols, anc_ref, count_ref, a_ref, f_ref, own_ref, held, factors, total, sems):
    half = rows // 2
    width = own_ref.shape[-1]
    step = 256
    loads = []
    for n in range(rows):
        load = pltpu.make_async_copy(f_ref.at[n], factors.at[n], sems.at[n])
        load.start()
        loads.append(load)
    me_row = lax.axis_index("prow")
    me_col = lax.axis_index("pcol")
    count = count_ref[me_col]
    row_live = (me_row < count).astype(jnp.float32)
    for n in range(rows):
        t = slot_row(me_row, n, rows)
        live = (t < count).astype(jnp.bfloat16)
        held[n] = a_ref[lax.rem(anc_ref[t, me_col], cols)] * live
    for n in range(0, rows, 2):
        for load in loads[n : n + 2]:
            load.wait()
        for q in range(width // step):
            at = pl.ds(q * step, step)
            part = jnp.dot(held[n], factors[n, :, at], preferred_element_type=jnp.float32)
            part += jnp.dot(held[n + 1], factors[n + 1, :, at], preferred_element_type=jnp.float32)
            if n > 0:
                part += total[:, at]
            if n < rows - 2:
                total[:, at] = part
            else:
                own_ref[:, at] = (part * -row_live).astype(jnp.bfloat16)


def slot_row(me_row, n, rows):
    half = rows // 2
    base = me_row if n < half else me_row + 1 - 2 * lax.rem(me_row, 2)
    return lax.rem(base - 2 * (n % half) + rows, rows)


def turn_kernel(rows, f_ref, out_ref, held, sems):
    half = rows // 2
    loads = [pltpu.make_async_copy(f_ref.at[n * half], held.at[n], sems.at[n]) for n in range(2)]
    for load in loads:
        load.start()
    for load in loads:
        load.wait()
    me = lax.axis_index("prow")
    y, core = me // 2, lax.rem(me, 2)
    for p, h in enumerate((2, 1 + 2 * core, 3 - 2 * core, 0)):
        at = pl.ds(pl.multiple_of((2 * lax.rem(y + h, half) + core) * SLICE, SLICE), SLICE)
        for n in range(2):
            out_ref[pl.ds(p * SLICE, SLICE), n * W : (n + 1) * W] = held[n, :, at].T


def term_kernel(base, turned_ref, own_ref, other_ref, *out_refs):
    for n, ref in enumerate(out_refs):
        at = pl.ds((base + n) * SLICE, SLICE)
        total = jnp.dot(turned_ref[at, 0:W], own_ref[...], preferred_element_type=jnp.float32)
        total += jnp.dot(turned_ref[at, W : 2 * W], other_ref[...], preferred_element_type=jnp.float32)
        ref[...] = total.astype(ref.dtype)


def store_kernel(own_ref, out_ref, sem):
    store = pltpu.make_async_copy(own_ref, out_ref, sem)
    store.start()
    store.wait()


def sum_kernel(diag_ref, kept_ref, *refs):
    total = kept_ref[...]
    for ref in refs[:-1]:
        total += ref[...].astype(jnp.float32)
    refs[-1][...] = diag_ref[...] - total


SMEM = pl.BlockSpec(memory_space=pltpu.SMEM)
VMEM = pl.BlockSpec(memory_space=pltpu.VMEM)
HBM = pl.BlockSpec(memory_space=pltpu.HBM)


def local(anc_inverse, factor_blocks, diag_in, ancestors, active_count):
    rows = lax.axis_size("prow")
    cols = lax.axis_size("pcol")
    chips = rows // 2
    width = factor_blocks.shape[-1]
    factor = factor_blocks[0, 0]
    lists = ancestors.T

    def shift(x, h):
        return lax.ppermute(x, "prow", [(i, (i + 2 * h) % rows) for i in range(rows)])

    def swap(x):
        return lax.ppermute(x, "prow", [(i, i ^ 1) for i in range(rows)])

    blocks = (anc_inverse.shape[0] // W) * (anc_inverse.shape[1] // W)
    sending = pl.pallas_call(
        functools.partial(pick_kernel, rows, cols),
        out_shape=jax.ShapeDtypeStruct((cols, W, W), jnp.bfloat16),
        in_specs=[HBM, HBM],
        out_specs=HBM,
        scratch_shapes=[
            pltpu.SMEM((rows, cols), jnp.int32),
            pltpu.VMEM((blocks, W, W), jnp.bfloat16),
            pltpu.SemaphoreType.DMA,
            pltpu.SemaphoreType.DMA((2, blocks)),
            pltpu.SemaphoreType.DMA((2, cols)),
        ],
        compiler_params=pltpu.CompilerParams(vmem_limit_bytes=60 * MIB),
        cost_estimate=pl.CostEstimate(flops=0, bytes_accessed=3 * MIB, transcendentals=0),
    )(lists, anc_inverse)
    arrived = lax.all_to_all(sending, "pcol", split_axis=0, concat_axis=0, tiled=True)

    same = jnp.stack([factor] + [shift(factor, h if h <= chips // 2 else h - chips) for h in range(1, chips)])
    factors = jnp.concatenate([same, swap(same)])
    turned = pl.pallas_call(
        functools.partial(turn_kernel, rows),
        out_shape=jax.ShapeDtypeStruct((chips * SLICE, 2 * W), jnp.bfloat16),
        in_specs=[HBM],
        out_specs=VMEM,
        scratch_shapes=[pltpu.VMEM((2, W, width), jnp.bfloat16), pltpu.SemaphoreType.DMA((2,))],
        compiler_params=pltpu.CompilerParams(vmem_limit_bytes=50 * MIB),
        cost_estimate=pl.CostEstimate(flops=0, bytes_accessed=2 * MIB, transcendentals=0),
    )(factors)
    arrived, turned = lax.optimization_barrier((arrived, turned))

    own = pl.pallas_call(
        functools.partial(product_kernel, rows, cols),
        out_shape=jax.ShapeDtypeStruct((W, width), jnp.bfloat16),
        in_specs=[SMEM, SMEM, VMEM, HBM],
        out_specs=VMEM,
        scratch_shapes=[
            pltpu.VMEM((rows, W, W), jnp.bfloat16),
            pltpu.VMEM((rows, W, width), jnp.bfloat16),
            pltpu.VMEM((W, width), jnp.float32),
            pltpu.SemaphoreType.DMA((rows,)),
        ],
        compiler_params=pltpu.CompilerParams(vmem_limit_bytes=50 * MIB),
        cost_estimate=pl.CostEstimate(flops=2 * rows * W * W * width, bytes_accessed=7 * MIB, transcendentals=0),
    )(lists, active_count, arrived, factors)
    other = swap(own)

    def terms(base, dtypes):
        return pl.pallas_call(
            functools.partial(term_kernel, base),
            out_shape=[jax.ShapeDtypeStruct((SLICE, width), dtype) for dtype in dtypes],
            in_specs=[VMEM] * 3,
            out_specs=[VMEM] * len(dtypes),
            compiler_params=pltpu.CompilerParams(vmem_limit_bytes=16 * MIB),
            cost_estimate=pl.CostEstimate(flops=4 * len(dtypes) * SLICE * W * width, bytes_accessed=2 * MIB, transcendentals=0),
        )(turned, own, other)

    def beside(x, way):
        pairs = []
        for i in range(rows):
            pairs.append((i, (i + way * (2 - 4 * (i % 2))) % rows))
        return lax.ppermute(x, "prow", pairs)

    (far,) = terms(0, [jnp.bfloat16])
    met = [shift(far, 2)]
    near, back, kept = terms(1, [jnp.bfloat16, jnp.bfloat16, jnp.float32])
    met += [beside(near, 1), beside(back, -1)]
    product = pl.pallas_call(
        store_kernel,
        out_shape=jax.ShapeDtypeStruct((W, width), jnp.bfloat16),
        in_specs=[VMEM],
        out_specs=HBM,
        scratch_shapes=[pltpu.SemaphoreType.DMA],
        compiler_params=pltpu.CompilerParams(vmem_limit_bytes=16 * MIB),
        cost_estimate=pl.CostEstimate(flops=0, bytes_accessed=MIB, transcendentals=0),
    )(own)
    diagonal = pl.pallas_call(
        sum_kernel,
        out_shape=jax.ShapeDtypeStruct((SLICE, width), jnp.float32),
        in_specs=[VMEM] * (chips + 1),
        out_specs=VMEM,
        compiler_params=pltpu.CompilerParams(vmem_limit_bytes=16 * MIB),
        cost_estimate=pl.CostEstimate(flops=0, bytes_accessed=2 * MIB, transcendentals=0),
    )(diag_in[0], kept, *met)
    return (product[None, None], diagonal[None])


def solution(mesh):
    placed = (
        P(("pole", "prow"), "pcol"),
        P(("pole", "pcol"), "prow", None, None),
        P(("pole", "pcol"), "prow", None),
        P(),
        P(),
    )
    return jax.shard_map(
        local,
        mesh=mesh,
        in_specs=placed,
        out_specs=(P(("pole", "pcol"), "prow", None, None), P(("pole", "pcol"), "prow", None)),
        check_vma=False,
    )
```

```python
import functools

import jax
import jax.numpy as jnp
from jax import lax
from jax.experimental import pallas as pl
from jax.experimental.pallas import tpu as pltpu
from jax.sharding import PartitionSpec as P

W = 256
SLICE = 128
MIB = 1024 * 1024


def pick_kernel(rows, cols, anc_ref, a_ref, out_ref, names, held, names_sem, in_sems, out_sems):
    high, wide = a_ref.shape[0] // W, a_ref.shape[1] // W
    part = W // 2
    fetch = pltpu.make_async_copy(anc_ref, names, names_sem)
    fetch.start()
    loads = []
    for p in range(2):
        for n in range(high * wide):
            i, j = n // wide, n % wide
            load = pltpu.make_async_copy(
                a_ref.at[pl.ds(i * W + p * part, part), pl.ds(j * W, W)],
                held.at[n, pl.ds(p * part, part)],
                in_sems.at[p, n],
            )
            load.start()
            loads.append(load)
    me_row = lax.axis_index("prow")
    me_col = lax.axis_index("pcol")
    slot = lax.rem(me_col, rows)
    fetch.wait()
    owed, picks = [], []
    for k in range(cols):
        name = names[slot, k]
        picks.append((names[me_row, k] // rows) * wide + name // cols)
        owed.append(lax.rem(name, cols) == me_col)
    stores = []
    for p in range(2):
        for load in loads[p * high * wide : (p + 1) * high * wide]:
            load.wait()
        at = pl.ds(p * part, part)
        for k in range(cols):
            store = pltpu.make_async_copy(held.at[picks[k], at], out_ref.at[k, at], out_sems.at[p, k])
            pl.when(owed[k])(store.start)
            stores.append((owed[k], store))
    for needed, store in stores:
        pl.when(needed)(store.wait)


def product_kernel(rows, cols, anc_ref, count_ref, a_ref, f_ref, own_ref, held, factors, total, sems, names, counts, small_sems):
    half = rows // 2
    width = own_ref.shape[-1]
    step = 256
    small = [
        pltpu.make_async_copy(anc_ref, names, small_sems.at[0]),
        pltpu.make_async_copy(count_ref, counts, small_sems.at[1]),
    ]
    for fetch in small:
        fetch.start()
    loads = []
    for n in range(rows):
        load = pltpu.make_async_copy(f_ref.at[n], factors.at[n], sems.at[n])
        load.start()
        loads.append(load)
    me_row = lax.axis_index("prow")
    me_col = lax.axis_index("pcol")
    for fetch in small:
        fetch.wait()
    count = counts[me_col]
    row_live = (me_row < count).astype(jnp.float32)
    for n in range(rows):
        t = slot_row(me_row, n, rows)
        live = (t < count).astype(jnp.bfloat16)
        held[n] = a_ref[lax.rem(names[t, me_col], cols)] * live
    for n in range(0, rows, 2):
        for load in loads[n : n + 2]:
            load.wait()
        for q in range(width // step):
            at = pl.ds(q * step, step)
            part = jnp.dot(held[n], factors[n, :, at], preferred_element_type=jnp.float32)
            part += jnp.dot(held[n + 1], factors[n + 1, :, at], preferred_element_type=jnp.float32)
            if n > 0:
                part += total[:, at]
            if n < rows - 2:
                total[:, at] = part
            else:
                own_ref[:, at] = (part * -row_live).astype(jnp.bfloat16)


def slot_row(me_row, n, rows):
    half = rows // 2
    base = me_row if n < half else me_row + 1 - 2 * lax.rem(me_row, 2)
    return lax.rem(base - 2 * (n % half) + rows, rows)


def turn_kernel(rows, f_ref, out_ref, held, sems):
    half = rows // 2
    loads = [pltpu.make_async_copy(f_ref.at[n * half], held.at[n], sems.at[n]) for n in range(2)]
    for load in loads:
        load.start()
    for load in loads:
        load.wait()
    me = lax.axis_index("prow")
    y, core = me // 2, lax.rem(me, 2)
    for p, h in enumerate((2, 1 + 2 * core, 3 - 2 * core, 0)):
        at = pl.ds(pl.multiple_of((2 * lax.rem(y + h, half) + core) * SLICE, SLICE), SLICE)
        for n in range(2):
            out_ref[pl.ds(p * SLICE, SLICE), n * W : (n + 1) * W] = held[n, :, at].T


def term_kernel(base, turned_ref, own_ref, other_ref, *out_refs):
    for n, ref in enumerate(out_refs):
        at = pl.ds((base + n) * SLICE, SLICE)
        total = jnp.dot(turned_ref[at, 0:W], own_ref[...], preferred_element_type=jnp.float32)
        total += jnp.dot(turned_ref[at, W : 2 * W], other_ref[...], preferred_element_type=jnp.float32)
        ref[...] = total.astype(ref.dtype)


def store_kernel(own_ref, out_ref, sem):
    store = pltpu.make_async_copy(own_ref, out_ref, sem)
    store.start()
    store.wait()


def sum_kernel(diag_ref, kept_ref, *refs):
    total = kept_ref[...]
    for ref in refs[:-1]:
        total += ref[...].astype(jnp.float32)
    refs[-1][...] = diag_ref[...] - total


SMEM = pl.BlockSpec(memory_space=pltpu.SMEM)
VMEM = pl.BlockSpec(memory_space=pltpu.VMEM)
HBM = pl.BlockSpec(memory_space=pltpu.HBM)


def local(anc_inverse, factor_blocks, diag_in, ancestors, active_count):
    rows = lax.axis_size("prow")
    cols = lax.axis_size("pcol")
    chips = rows // 2
    width = factor_blocks.shape[-1]
    factor = factor_blocks[0, 0]
    lists = ancestors.T

    def shift(x, h):
        return lax.ppermute(x, "prow", [(i, (i + 2 * h) % rows) for i in range(rows)])

    def swap(x):
        return lax.ppermute(x, "prow", [(i, i ^ 1) for i in range(rows)])

    blocks = (anc_inverse.shape[0] // W) * (anc_inverse.shape[1] // W)
    sending = pl.pallas_call(
        functools.partial(pick_kernel, rows, cols),
        out_shape=jax.ShapeDtypeStruct((cols, W, W), jnp.bfloat16),
        in_specs=[HBM, HBM],
        out_specs=HBM,
        scratch_shapes=[
            pltpu.SMEM((rows, cols), jnp.int32),
            pltpu.VMEM((blocks, W, W), jnp.bfloat16),
            pltpu.SemaphoreType.DMA,
            pltpu.SemaphoreType.DMA((2, blocks)),
            pltpu.SemaphoreType.DMA((2, cols)),
        ],
        compiler_params=pltpu.CompilerParams(vmem_limit_bytes=60 * MIB),
        cost_estimate=pl.CostEstimate(flops=0, bytes_accessed=3 * MIB, transcendentals=0),
    )(lists, anc_inverse)
    arrived = lax.all_to_all(sending, "pcol", split_axis=0, concat_axis=0, tiled=True)

    same = jnp.stack([factor] + [shift(factor, h if h <= chips // 2 else h - chips) for h in range(1, chips)])
    factors = jnp.concatenate([same, swap(same)])
    turned = pl.pallas_call(
        functools.partial(turn_kernel, rows),
        out_shape=jax.ShapeDtypeStruct((chips * SLICE, 2 * W), jnp.bfloat16),
        in_specs=[HBM],
        out_specs=VMEM,
        scratch_shapes=[pltpu.VMEM((2, W, width), jnp.bfloat16), pltpu.SemaphoreType.DMA((2,))],
        compiler_params=pltpu.CompilerParams(vmem_limit_bytes=50 * MIB),
        cost_estimate=pl.CostEstimate(flops=0, bytes_accessed=2 * MIB, transcendentals=0),
    )(factors)
    arrived, turned = lax.optimization_barrier((arrived, turned))

    own = pl.pallas_call(
        functools.partial(product_kernel, rows, cols),
        out_shape=jax.ShapeDtypeStruct((W, width), jnp.bfloat16),
        in_specs=[HBM, HBM, VMEM, HBM],
        out_specs=VMEM,
        scratch_shapes=[
            pltpu.VMEM((rows, W, W), jnp.bfloat16),
            pltpu.VMEM((rows, W, width), jnp.bfloat16),
            pltpu.VMEM((W, width), jnp.float32),
            pltpu.SemaphoreType.DMA((rows,)),
            pltpu.SMEM((rows, cols), jnp.int32),
            pltpu.SMEM((cols,), jnp.int32),
            pltpu.SemaphoreType.DMA((2,)),
        ],
        compiler_params=pltpu.CompilerParams(vmem_limit_bytes=50 * MIB),
        cost_estimate=pl.CostEstimate(flops=2 * rows * W * W * width, bytes_accessed=7 * MIB, transcendentals=0),
    )(lists, active_count, arrived, factors)
    other = swap(own)

    def terms(base, dtypes):
        return pl.pallas_call(
            functools.partial(term_kernel, base),
            out_shape=[jax.ShapeDtypeStruct((SLICE, width), dtype) for dtype in dtypes],
            in_specs=[VMEM] * 3,
            out_specs=[VMEM] * len(dtypes),
            compiler_params=pltpu.CompilerParams(vmem_limit_bytes=16 * MIB),
            cost_estimate=pl.CostEstimate(flops=4 * len(dtypes) * SLICE * W * width, bytes_accessed=2 * MIB, transcendentals=0),
        )(turned, own, other)

    def beside(x, way):
        pairs = []
        for i in range(rows):
            pairs.append((i, (i + way * (2 - 4 * (i % 2))) % rows))
        return lax.ppermute(x, "prow", pairs)

    (far,) = terms(0, [jnp.bfloat16])
    met = [shift(far, 2)]
    near, back, kept = terms(1, [jnp.bfloat16, jnp.bfloat16, jnp.float32])
    met += [beside(near, 1), beside(back, -1)]
    product = pl.pallas_call(
        store_kernel,
        out_shape=jax.ShapeDtypeStruct((W, width), jnp.bfloat16),
        in_specs=[VMEM],
        out_specs=HBM,
        scratch_shapes=[pltpu.SemaphoreType.DMA],
        compiler_params=pltpu.CompilerParams(vmem_limit_bytes=16 * MIB),
        cost_estimate=pl.CostEstimate(flops=0, bytes_accessed=MIB, transcendentals=0),
    )(own)
    diagonal = pl.pallas_call(
        sum_kernel,
        out_shape=jax.ShapeDtypeStruct((SLICE, width), jnp.float32),
        in_specs=[VMEM] * (chips + 1),
        out_specs=VMEM,
        compiler_params=pltpu.CompilerParams(vmem_limit_bytes=16 * MIB),
        cost_estimate=pl.CostEstimate(flops=0, bytes_accessed=2 * MIB, transcendentals=0),
    )(diag_in[0], kept, *met)
    return (product[None, None], diagonal[None])


def solution(mesh):
    placed = (
        P(("pole", "prow"), "pcol"),
        P(("pole", "pcol"), "prow", None, None),
        P(("pole", "pcol"), "prow", None),
        P(),
        P(),
    )
    return jax.shard_map(
        local,
        mesh=mesh,
        in_specs=placed,
        out_specs=(P(("pole", "pcol"), "prow", None, None), P(("pole", "pcol"), "prow", None)),
        check_vma=False,
    )
```

```python
import functools

import jax
import jax.numpy as jnp
from jax import lax
from jax.experimental import pallas as pl
from jax.experimental.pallas import tpu as pltpu
from jax.sharding import PartitionSpec as P

W = 256
SLICE = 128
MIB = 1024 * 1024


def pick_kernel(rows, cols, anc_ref, a_ref, out_ref, names, held, names_sem, in_sems, out_sems):
    fetch = pltpu.make_async_copy(anc_ref, names, names_sem)
    fetch.start()
    loads = []
    for i in range(a_ref.shape[0] // W):
        at = pl.ds(i * W, W)
        load = pltpu.make_async_copy(a_ref.at[at], held.at[at], in_sems.at[i])
        load.start()
        loads.append(load)
    me_row = lax.axis_index("prow")
    me_col = lax.axis_index("pcol")
    slot = lax.rem(me_col, rows)
    fetch.wait()
    stores = []
    for k in range(cols):
        name = names[slot, k]
        i = names[me_row, k] // rows
        j = name // cols
        block = held.at[pl.ds(pl.multiple_of(i * W, W), W), pl.ds(pl.multiple_of(j * W, W), W)]
        stores.append((lax.rem(name, cols) == me_col, pltpu.make_async_copy(block, out_ref.at[k], out_sems.at[k])))
    for load in loads:
        load.wait()
    for owed, store in stores:
        pl.when(owed)(store.start)
    for owed, store in stores:
        pl.when(owed)(store.wait)


def product_kernel(rows, cols, anc_ref, count_ref, a_ref, f_ref, own_ref, held, factors, total, sems, names, counts, small_sems):
    half = rows // 2
    width = own_ref.shape[-1]
    step = 256
    small = [
        pltpu.make_async_copy(anc_ref, names, small_sems.at[0]),
        pltpu.make_async_copy(count_ref, counts, small_sems.at[1]),
    ]
    for fetch in small:
        fetch.start()
    loads = []
    for n in range(rows):
        load = pltpu.make_async_copy(f_ref.at[n], factors.at[n], sems.at[n])
        load.start()
        loads.append(load)
    me_row = lax.axis_index("prow")
    me_col = lax.axis_index("pcol")
    for fetch in small:
        fetch.wait()
    count = counts[me_col]
    row_live = (me_row < count).astype(jnp.float32)
    for n in range(rows):
        t = slot_row(me_row, n, rows)
        live = (t < count).astype(jnp.bfloat16)
        held[n] = a_ref[lax.rem(names[t, me_col], cols)] * live
    for n in range(0, rows, 2):
        for load in loads[n : n + 2]:
            load.wait()
        for q in range(width // step):
            at = pl.ds(q * step, step)
            part = jnp.dot(held[n], factors[n, :, at], preferred_element_type=jnp.float32)
            part += jnp.dot(held[n + 1], factors[n + 1, :, at], preferred_element_type=jnp.float32)
            if n > 0:
                part += total[:, at]
            if n < rows - 2:
                total[:, at] = part
            else:
                own_ref[:, at] = (part * -row_live).astype(jnp.bfloat16)


def slot_row(me_row, n, rows):
    half = rows // 2
    base = me_row if n < half else me_row + 1 - 2 * lax.rem(me_row, 2)
    return lax.rem(base - 2 * (n % half) + rows, rows)


def turn_kernel(rows, f_ref, out_ref, held, sems):
    half = rows // 2
    loads = [pltpu.make_async_copy(f_ref.at[n * half], held.at[n], sems.at[n]) for n in range(2)]
    for load in loads:
        load.start()
    for load in loads:
        load.wait()
    me = lax.axis_index("prow")
    y, core = me // 2, lax.rem(me, 2)
    for p, h in enumerate((2, 1 + 2 * core, 3 - 2 * core, 0)):
        at = pl.ds(pl.multiple_of((2 * lax.rem(y + h, half) + core) * SLICE, SLICE), SLICE)
        for n in range(2):
            out_ref[pl.ds(p * SLICE, SLICE), n * W : (n + 1) * W] = held[n, :, at].T


def term_kernel(base, turned_ref, own_ref, other_ref, *out_refs):
    for n, ref in enumerate(out_refs):
        at = pl.ds((base + n) * SLICE, SLICE)
        total = jnp.dot(turned_ref[at, 0:W], own_ref[...], preferred_element_type=jnp.float32)
        total += jnp.dot(turned_ref[at, W : 2 * W], other_ref[...], preferred_element_type=jnp.float32)
        ref[...] = total.astype(ref.dtype)


def store_kernel(own_ref, diag_ref, kept_ref, out_ref, base_ref, sem):
    store = pltpu.make_async_copy(own_ref, out_ref, sem)
    store.start()
    base_ref[...] = diag_ref[...] - kept_ref[...]
    store.wait()


def sum_kernel(base_ref, *refs):
    out_ref, held, sems = refs[-3:]
    part = SLICE // 4
    stores = []
    for p in range(4):
        at = pl.ds(p * part, part)
        total = base_ref[at]
        for ref in refs[:-3]:
            total -= ref[at].astype(jnp.float32)
        held[at] = total
        store = pltpu.make_async_copy(held.at[at], out_ref.at[at], sems.at[p])
        store.start()
        stores.append(store)
    for store in stores:
        store.wait()


SMEM = pl.BlockSpec(memory_space=pltpu.SMEM)
VMEM = pl.BlockSpec(memory_space=pltpu.VMEM)
HBM = pl.BlockSpec(memory_space=pltpu.HBM)


def local(anc_inverse, factor_blocks, diag_in, ancestors, active_count):
    rows = lax.axis_size("prow")
    cols = lax.axis_size("pcol")
    chips = rows // 2
    width = factor_blocks.shape[-1]
    factor = factor_blocks[0, 0]
    lists = ancestors.T

    def shift(x, h):
        return lax.ppermute(x, "prow", [(i, (i + 2 * h) % rows) for i in range(rows)])

    def swap(x):
        return lax.ppermute(x, "prow", [(i, i ^ 1) for i in range(rows)])

    sending = pl.pallas_call(
        functools.partial(pick_kernel, rows, cols),
        out_shape=jax.ShapeDtypeStruct((cols, W, W), jnp.bfloat16),
        in_specs=[HBM, HBM],
        out_specs=HBM,
        scratch_shapes=[
            pltpu.SMEM((rows, cols), jnp.int32),
            pltpu.VMEM(anc_inverse.shape, jnp.bfloat16),
            pltpu.SemaphoreType.DMA,
            pltpu.SemaphoreType.DMA((anc_inverse.shape[0] // W,)),
            pltpu.SemaphoreType.DMA((cols,)),
        ],
        compiler_params=pltpu.CompilerParams(vmem_limit_bytes=60 * MIB),
        cost_estimate=pl.CostEstimate(flops=0, bytes_accessed=3 * MIB, transcendentals=0),
    )(lists, anc_inverse)
    arrived = lax.all_to_all(sending, "pcol", split_axis=0, concat_axis=0, tiled=True)

    same = jnp.stack([factor] + [shift(factor, h if h <= chips // 2 else h - chips) for h in range(1, chips)])
    factors = jnp.concatenate([same, swap(same)])
    turned = pl.pallas_call(
        functools.partial(turn_kernel, rows),
        out_shape=jax.ShapeDtypeStruct((chips * SLICE, 2 * W), jnp.bfloat16),
        in_specs=[HBM],
        out_specs=VMEM,
        scratch_shapes=[pltpu.VMEM((2, W, width), jnp.bfloat16), pltpu.SemaphoreType.DMA((2,))],
        compiler_params=pltpu.CompilerParams(vmem_limit_bytes=50 * MIB),
        cost_estimate=pl.CostEstimate(flops=0, bytes_accessed=2 * MIB, transcendentals=0),
    )(factors)
    arrived, turned = lax.optimization_barrier((arrived, turned))

    own = pl.pallas_call(
        functools.partial(product_kernel, rows, cols),
        out_shape=jax.ShapeDtypeStruct((W, width), jnp.bfloat16),
        in_specs=[HBM, HBM, VMEM, HBM],
        out_specs=VMEM,
        scratch_shapes=[
            pltpu.VMEM((rows, W, W), jnp.bfloat16),
            pltpu.VMEM((rows, W, width), jnp.bfloat16),
            pltpu.VMEM((W, width), jnp.float32),
            pltpu.SemaphoreType.DMA((rows,)),
            pltpu.SMEM((rows, cols), jnp.int32),
            pltpu.SMEM((cols,), jnp.int32),
            pltpu.SemaphoreType.DMA((2,)),
        ],
        compiler_params=pltpu.CompilerParams(vmem_limit_bytes=50 * MIB),
        cost_estimate=pl.CostEstimate(flops=2 * rows * W * W * width, bytes_accessed=7 * MIB, transcendentals=0),
    )(lists, active_count, arrived, factors)
    other = swap(own)

    def terms(base, dtypes):
        return pl.pallas_call(
            functools.partial(term_kernel, base),
            out_shape=[jax.ShapeDtypeStruct((SLICE, width), dtype) for dtype in dtypes],
            in_specs=[VMEM] * 3,
            out_specs=[VMEM] * len(dtypes),
            compiler_params=pltpu.CompilerParams(vmem_limit_bytes=16 * MIB),
            cost_estimate=pl.CostEstimate(flops=4 * len(dtypes) * SLICE * W * width, bytes_accessed=2 * MIB, transcendentals=0),
        )(turned, own, other)

    def beside(x, way):
        pairs = []
        for i in range(rows):
            pairs.append((i, (i + way * (2 - 4 * (i % 2))) % rows))
        return lax.ppermute(x, "prow", pairs)

    (far,) = terms(0, [jnp.bfloat16])
    met = [shift(far, 2)]
    near, back, kept = terms(1, [jnp.bfloat16, jnp.bfloat16, jnp.float32])
    met += [beside(near, 1), beside(back, -1)]
    product, base = pl.pallas_call(
        store_kernel,
        out_shape=(jax.ShapeDtypeStruct((W, width), jnp.bfloat16), jax.ShapeDtypeStruct((SLICE, width), jnp.float32)),
        in_specs=[VMEM] * 3,
        out_specs=(HBM, VMEM),
        scratch_shapes=[pltpu.SemaphoreType.DMA],
        compiler_params=pltpu.CompilerParams(vmem_limit_bytes=16 * MIB),
        cost_estimate=pl.CostEstimate(flops=0, bytes_accessed=2 * MIB, transcendentals=0),
    )(own, diag_in[0], kept)
    diagonal = pl.pallas_call(
        sum_kernel,
        out_shape=jax.ShapeDtypeStruct((SLICE, width), jnp.float32),
        in_specs=[VMEM] * chips,
        out_specs=HBM,
        scratch_shapes=[pltpu.VMEM((SLICE, width), jnp.float32), pltpu.SemaphoreType.DMA((4,))],
        compiler_params=pltpu.CompilerParams(vmem_limit_bytes=16 * MIB),
        cost_estimate=pl.CostEstimate(flops=0, bytes_accessed=2 * MIB, transcendentals=0),
    )(base, *met)
    return (product[None, None], diagonal[None])


def solution(mesh):
    placed = (
        P(("pole", "prow"), "pcol"),
        P(("pole", "pcol"), "prow", None, None),
        P(("pole", "pcol"), "prow", None),
        P(),
        P(),
    )
    return jax.shard_map(
        local,
        mesh=mesh,
        in_specs=placed,
        out_specs=(P(("pole", "pcol"), "prow", None, None), P(("pole", "pcol"), "prow", None)),
        check_vma=False,
    )
```

```python
import functools

import jax
import jax.numpy as jnp
from jax import lax
from jax.experimental import pallas as pl
from jax.experimental.pallas import tpu as pltpu
from jax.sharding import PartitionSpec as P

W = 256
SLICE = 128
MIB = 1024 * 1024


def pick_kernel(rows, cols, anc_ref, a_ref, out_ref, names, held, names_sem, in_sems, out_sems):
    fetch = pltpu.make_async_copy(anc_ref, names, names_sem)
    fetch.start()
    loads = []
    for i in range(a_ref.shape[0] // W):
        at = pl.ds(i * W, W)
        load = pltpu.make_async_copy(a_ref.at[at], held.at[at], in_sems.at[i])
        load.start()
        loads.append(load)
    me_row = lax.axis_index("prow")
    me_col = lax.axis_index("pcol")
    slot = lax.rem(me_col, rows)
    fetch.wait()
    stores = []
    for k in range(cols):
        name = names[slot, k]
        i = names[me_row, k] // rows
        j = name // cols
        block = held.at[pl.ds(pl.multiple_of(i * W, W), W), pl.ds(pl.multiple_of(j * W, W), W)]
        stores.append((lax.rem(name, cols) == me_col, pltpu.make_async_copy(block, out_ref.at[k], out_sems.at[k])))
    for load in loads:
        load.wait()
    for owed, store in stores:
        pl.when(owed)(store.start)
    for owed, store in stores:
        pl.when(owed)(store.wait)


def product_kernel(rows, cols, anc_ref, count_ref, a_ref, mine_ref, f_ref, own_ref, held, factors, total, sems, names, counts, small_sems):
    width = own_ref.shape[-1]
    step = 256
    small = [
        pltpu.make_async_copy(anc_ref, names, small_sems.at[0]),
        pltpu.make_async_copy(count_ref, counts, small_sems.at[1]),
    ]
    for fetch in small:
        fetch.start()
    loads = []
    for n in range(1, rows):
        load = pltpu.make_async_copy(f_ref.at[n], factors.at[pl.ds((n - 1) * W, W)], sems.at[n - 1])
        load.start()
        loads.append(load)
    me_row = lax.axis_index("prow")
    me_col = lax.axis_index("pcol")
    for fetch in small:
        fetch.wait()
    count = counts[me_col]
    row_live = (me_row < count).astype(jnp.float32)

    def hold(n):
        t = slot_row(me_row, n, rows)
        live = (t < count).astype(jnp.bfloat16)
        held[:, n * W : (n + 1) * W] = a_ref[lax.rem(names[t, me_col], cols)] * live

    hold(0)
    for q in range(width // step):
        at = pl.ds(q * step, step)
        total[:, at] = jnp.dot(held[:, 0:W], mine_ref[:, at], preferred_element_type=jnp.float32)
    for n in range(1, rows):
        hold(n)
    for n in range(1, rows, 2):
        size = min(2, rows - n)
        for load in loads[n - 1 : n - 1 + size]:
            load.wait()
        for q in range(width // step):
            at = pl.ds(q * step, step)
            part = total[:, at] + jnp.dot(
                held[:, n * W : (n + size) * W],
                factors[(n - 1) * W : (n - 1 + size) * W, at],
                preferred_element_type=jnp.float32,
            )
            if n + size < rows:
                total[:, at] = part
            else:
                own_ref[:, at] = (part * -row_live).astype(jnp.bfloat16)


def slot_row(me_row, n, rows):
    half = rows // 2
    base = me_row if n < half else me_row + 1 - 2 * lax.rem(me_row, 2)
    return lax.rem(base - 2 * (n % half) + rows, rows)


def turn_kernel(rows, f_ref, out_ref, held, sems):
    half = rows // 2
    loads = [pltpu.make_async_copy(f_ref.at[n * half], held.at[n], sems.at[n]) for n in range(2)]
    for load in loads:
        load.start()
    for load in loads:
        load.wait()
    me = lax.axis_index("prow")
    y, core = me // 2, lax.rem(me, 2)
    for p, h in enumerate((2, 1 + 2 * core, 3 - 2 * core, 0)):
        at = pl.ds(pl.multiple_of((2 * lax.rem(y + h, half) + core) * SLICE, SLICE), SLICE)
        for n in range(2):
            out_ref[pl.ds(p * SLICE, SLICE), n * W : (n + 1) * W] = held[n, :, at].T


def term_kernel(base, turned_ref, own_ref, other_ref, *out_refs):
    for n, ref in enumerate(out_refs):
        at = pl.ds((base + n) * SLICE, SLICE)
        total = jnp.dot(turned_ref[at, 0:W], own_ref[...], preferred_element_type=jnp.float32)
        total += jnp.dot(turned_ref[at, W : 2 * W], other_ref[...], preferred_element_type=jnp.float32)
        ref[...] = total.astype(ref.dtype)


def store_kernel(own_ref, diag_ref, kept_ref, out_ref, base_ref, sem):
    store = pltpu.make_async_copy(own_ref, out_ref, sem)
    store.start()
    base_ref[...] = diag_ref[...] - kept_ref[...]
    store.wait()


def sum_kernel(base_ref, *refs):
    out_ref, held, sems = refs[-3:]
    part = SLICE // 4
    stores = []
    for p in range(4):
        at = pl.ds(p * part, part)
        total = base_ref[at]
        for ref in refs[:-3]:
            total -= ref[at].astype(jnp.float32)
        held[at] = total
        store = pltpu.make_async_copy(held.at[at], out_ref.at[at], sems.at[p])
        store.start()
        stores.append(store)
    for store in stores:
        store.wait()


SMEM = pl.BlockSpec(memory_space=pltpu.SMEM)
VMEM = pl.BlockSpec(memory_space=pltpu.VMEM)
HBM = pl.BlockSpec(memory_space=pltpu.HBM)


def local(anc_inverse, factor_blocks, diag_in, ancestors, active_count):
    rows = lax.axis_size("prow")
    cols = lax.axis_size("pcol")
    chips = rows // 2
    width = factor_blocks.shape[-1]
    factor = factor_blocks[0, 0]
    lists = ancestors.T

    def shift(x, h):
        return lax.ppermute(x, "prow", [(i, (i + 2 * h) % rows) for i in range(rows)])

    def swap(x):
        return lax.ppermute(x, "prow", [(i, i ^ 1) for i in range(rows)])

    sending = pl.pallas_call(
        functools.partial(pick_kernel, rows, cols),
        out_shape=jax.ShapeDtypeStruct((cols, W, W), jnp.bfloat16),
        in_specs=[HBM, HBM],
        out_specs=HBM,
        scratch_shapes=[
            pltpu.SMEM((rows, cols), jnp.int32),
            pltpu.VMEM(anc_inverse.shape, jnp.bfloat16),
            pltpu.SemaphoreType.DMA,
            pltpu.SemaphoreType.DMA((anc_inverse.shape[0] // W,)),
            pltpu.SemaphoreType.DMA((cols,)),
        ],
        compiler_params=pltpu.CompilerParams(vmem_limit_bytes=60 * MIB),
        cost_estimate=pl.CostEstimate(flops=0, bytes_accessed=3 * MIB, transcendentals=0),
    )(lists, anc_inverse)
    arrived = lax.all_to_all(sending, "pcol", split_axis=0, concat_axis=0, tiled=True)

    same = jnp.stack([factor] + [shift(factor, h if h <= chips // 2 else h - chips) for h in range(1, chips)])
    factors = jnp.concatenate([same, swap(same)])
    turned = pl.pallas_call(
        functools.partial(turn_kernel, rows),
        out_shape=jax.ShapeDtypeStruct((chips * SLICE, 2 * W), jnp.bfloat16),
        in_specs=[HBM],
        out_specs=VMEM,
        scratch_shapes=[pltpu.VMEM((2, W, width), jnp.bfloat16), pltpu.SemaphoreType.DMA((2,))],
        compiler_params=pltpu.CompilerParams(vmem_limit_bytes=50 * MIB),
        cost_estimate=pl.CostEstimate(flops=0, bytes_accessed=2 * MIB, transcendentals=0),
    )(factors)
    arrived, turned = lax.optimization_barrier((arrived, turned))

    own = pl.pallas_call(
        functools.partial(product_kernel, rows, cols),
        out_shape=jax.ShapeDtypeStruct((W, width), jnp.bfloat16),
        in_specs=[HBM, HBM, VMEM, VMEM, HBM],
        out_specs=VMEM,
        scratch_shapes=[
            pltpu.VMEM((W, rows * W), jnp.bfloat16),
            pltpu.VMEM(((rows - 1) * W, width), jnp.bfloat16),
            pltpu.VMEM((W, width), jnp.float32),
            pltpu.SemaphoreType.DMA((rows - 1,)),
            pltpu.SMEM((rows, cols), jnp.int32),
            pltpu.SMEM((cols,), jnp.int32),
            pltpu.SemaphoreType.DMA((2,)),
        ],
        compiler_params=pltpu.CompilerParams(vmem_limit_bytes=50 * MIB),
        cost_estimate=pl.CostEstimate(flops=2 * rows * W * W * width, bytes_accessed=7 * MIB, transcendentals=0),
    )(lists, active_count, arrived, factor, factors)
    other = swap(own)

    def terms(base, dtypes):
        return pl.pallas_call(
            functools.partial(term_kernel, base),
            out_shape=[jax.ShapeDtypeStruct((SLICE, width), dtype) for dtype in dtypes],
            in_specs=[VMEM] * 3,
            out_specs=[VMEM] * len(dtypes),
            compiler_params=pltpu.CompilerParams(vmem_limit_bytes=16 * MIB),
            cost_estimate=pl.CostEstimate(flops=4 * len(dtypes) * SLICE * W * width, bytes_accessed=2 * MIB, transcendentals=0),
        )(turned, own, other)

    def beside(x, way):
        pairs = []
        for i in range(rows):
            pairs.append((i, (i + way * (2 - 4 * (i % 2))) % rows))
        return lax.ppermute(x, "prow", pairs)

    (far,) = terms(0, [jnp.bfloat16])
    met = [shift(far, 2)]
    near, back, kept = terms(1, [jnp.bfloat16, jnp.bfloat16, jnp.float32])
    met += [beside(near, 1), beside(back, -1)]
    product, base = pl.pallas_call(
        store_kernel,
        out_shape=(jax.ShapeDtypeStruct((W, width), jnp.bfloat16), jax.ShapeDtypeStruct((SLICE, width), jnp.float32)),
        in_specs=[VMEM] * 3,
        out_specs=(HBM, VMEM),
        scratch_shapes=[pltpu.SemaphoreType.DMA],
        compiler_params=pltpu.CompilerParams(vmem_limit_bytes=16 * MIB),
        cost_estimate=pl.CostEstimate(flops=0, bytes_accessed=2 * MIB, transcendentals=0),
    )(own, diag_in[0], kept)
    diagonal = pl.pallas_call(
        sum_kernel,
        out_shape=jax.ShapeDtypeStruct((SLICE, width), jnp.float32),
        in_specs=[VMEM] * chips,
        out_specs=HBM,
        scratch_shapes=[pltpu.VMEM((SLICE, width), jnp.float32), pltpu.SemaphoreType.DMA((4,))],
        compiler_params=pltpu.CompilerParams(vmem_limit_bytes=16 * MIB),
        cost_estimate=pl.CostEstimate(flops=0, bytes_accessed=2 * MIB, transcendentals=0),
    )(base, *met)
    return (product[None, None], diagonal[None])


def solution(mesh):
    placed = (
        P(("pole", "prow"), "pcol"),
        P(("pole", "pcol"), "prow", None, None),
        P(("pole", "pcol"), "prow", None),
        P(),
        P(),
    )
    return jax.shard_map(
        local,
        mesh=mesh,
        in_specs=placed,
        out_specs=(P(("pole", "pcol"), "prow", None, None), P(("pole", "pcol"), "prow", None)),
        check_vma=False,
    )
```

```python
import functools

import jax
import jax.numpy as jnp
from jax import lax
from jax.experimental import pallas as pl
from jax.experimental.pallas import tpu as pltpu
from jax.sharding import PartitionSpec as P

W = 256
SLICE = 128
MIB = 1024 * 1024


def pick_kernel(rows, cols, anc_ref, a_ref, out_ref, names, held, names_sem, in_sems, out_sems):
    fetch = pltpu.make_async_copy(anc_ref, names, names_sem)
    fetch.start()
    loads = []
    for i in range(a_ref.shape[0] // W):
        at = pl.ds(i * W, W)
        load = pltpu.make_async_copy(a_ref.at[at], held.at[at], in_sems.at[i])
        load.start()
        loads.append(load)
    me_row = lax.axis_index("prow")
    me_col = lax.axis_index("pcol")
    slot = lax.rem(me_col, rows)
    fetch.wait()
    stores = []
    for k in range(cols):
        name = names[slot, k]
        i = names[me_row, k] // rows
        j = name // cols
        block = held.at[pl.ds(pl.multiple_of(i * W, W), W), pl.ds(pl.multiple_of(j * W, W), W)]
        stores.append((lax.rem(name, cols) == me_col, pltpu.make_async_copy(block, out_ref.at[k], out_sems.at[k])))
    for load in loads:
        load.wait()
    for owed, store in stores:
        pl.when(owed)(store.start)
    for owed, store in stores:
        pl.when(owed)(store.wait)


def product_kernel(rows, cols, anc_ref, count_ref, a_ref, mine_ref, f_ref, own_ref, held, factors, total, sems, names, counts, small_sems):
    width = own_ref.shape[-1]
    step = 256
    small = [
        pltpu.make_async_copy(anc_ref, names, small_sems.at[0]),
        pltpu.make_async_copy(count_ref, counts, small_sems.at[1]),
    ]
    for fetch in small:
        fetch.start()
    loads = []
    for n in range(1, rows):
        load = pltpu.make_async_copy(f_ref.at[n], factors.at[pl.ds((n - 1) * W, W)], sems.at[n - 1])
        load.start()
        loads.append(load)
    me_row = lax.axis_index("prow")
    me_col = lax.axis_index("pcol")
    for fetch in small:
        fetch.wait()
    count = counts[me_col]
    row_live = (me_row < count).astype(jnp.float32)

    def hold(n):
        t = slot_row(me_row, n, rows)
        live = (t < count).astype(jnp.bfloat16)
        held[:, n * W : (n + 1) * W] = a_ref[lax.rem(names[t, me_col], cols)] * live

    hold(0)
    for q in range(width // step):
        at = pl.ds(q * step, step)
        total[:, at] = jnp.dot(held[:, 0:W], mine_ref[:, at], preferred_element_type=jnp.float32)
    for n in range(1, rows):
        hold(n)
    for n in range(1, rows, 2):
        size = min(2, rows - n)
        for load in loads[n - 1 : n - 1 + size]:
            load.wait()
        for q in range(width // step):
            at = pl.ds(q * step, step)
            part = total[:, at] + jnp.dot(
                held[:, n * W : (n + size) * W],
                factors[(n - 1) * W : (n - 1 + size) * W, at],
                preferred_element_type=jnp.float32,
            )
            if n + size < rows:
                total[:, at] = part
            else:
                own_ref[:, at] = (part * -row_live).astype(jnp.bfloat16)


def slot_row(me_row, n, rows):
    half = rows // 2
    base = me_row if n < half else me_row + 1 - 2 * lax.rem(me_row, 2)
    return lax.rem(base - 2 * (n % half) + rows, rows)


def turn_kernel(rows, f_ref, out_ref, held, sems):
    half = rows // 2
    loads = [pltpu.make_async_copy(f_ref.at[n * half], held.at[n], sems.at[n]) for n in range(2)]
    for load in loads:
        load.start()
    for load in loads:
        load.wait()
    me = lax.axis_index("prow")
    y, core = me // 2, lax.rem(me, 2)
    for p, h in enumerate((2, 1 + 2 * core, 3 - 2 * core, 0)):
        at = pl.ds(pl.multiple_of((2 * lax.rem(y + h, half) + core) * SLICE, SLICE), SLICE)
        for n in range(2):
            out_ref[pl.ds(p * SLICE, SLICE), n * W : (n + 1) * W] = held[n, :, at].T


def term_kernel(base, turned_ref, own_ref, other_ref, *out_refs):
    for n, ref in enumerate(out_refs):
        at = pl.ds((base + n) * SLICE, SLICE)
        total = jnp.dot(turned_ref[at, 0:W], own_ref[...], preferred_element_type=jnp.float32)
        total += jnp.dot(turned_ref[at, W : 2 * W], other_ref[...], preferred_element_type=jnp.float32)
        ref[...] = total.astype(ref.dtype)


def store_kernel(own_ref, diag_ref, kept_ref, out_ref, base_ref, sem):
    store = pltpu.make_async_copy(own_ref, out_ref, sem)
    store.start()
    base_ref[...] = diag_ref[...] - kept_ref[...]
    store.wait()


def sum_kernel(base_ref, *refs):
    out_ref, held, sems = refs[-3:]
    part = SLICE // 4
    stores = []
    for p in range(4):
        at = pl.ds(p * part, part)
        total = base_ref[at]
        for ref in refs[:-3]:
            total -= ref[at].astype(jnp.float32)
        held[at] = total
        store = pltpu.make_async_copy(held.at[at], out_ref.at[at], sems.at[p])
        store.start()
        stores.append(store)
    for store in stores:
        store.wait()


SMEM = pl.BlockSpec(memory_space=pltpu.SMEM)
VMEM = pl.BlockSpec(memory_space=pltpu.VMEM)
HBM = pl.BlockSpec(memory_space=pltpu.HBM)


def local(anc_inverse, factor_blocks, diag_in, ancestors, active_count):
    rows = lax.axis_size("prow")
    cols = lax.axis_size("pcol")
    chips = rows // 2
    width = factor_blocks.shape[-1]
    factor = factor_blocks[0, 0]
    lists = ancestors.T

    def shift(x, h):
        return lax.ppermute(x, "prow", [(i, (i + 2 * h) % rows) for i in range(rows)])

    def swap(x):
        return lax.ppermute(x, "prow", [(i, i ^ 1) for i in range(rows)])

    sending = pl.pallas_call(
        functools.partial(pick_kernel, rows, cols),
        out_shape=jax.ShapeDtypeStruct((cols, W, W), jnp.bfloat16),
        in_specs=[HBM, HBM],
        out_specs=HBM,
        scratch_shapes=[
            pltpu.SMEM((rows, cols), jnp.int32),
            pltpu.VMEM(anc_inverse.shape, jnp.bfloat16),
            pltpu.SemaphoreType.DMA,
            pltpu.SemaphoreType.DMA((anc_inverse.shape[0] // W,)),
            pltpu.SemaphoreType.DMA((cols,)),
        ],
        compiler_params=pltpu.CompilerParams(vmem_limit_bytes=60 * MIB),
        cost_estimate=pl.CostEstimate(flops=0, bytes_accessed=3 * MIB, transcendentals=0),
    )(lists, anc_inverse)
    arrived = lax.all_to_all(sending, "pcol", split_axis=0, concat_axis=0, tiled=True)

    same = jnp.stack([factor] + [shift(factor, h if h <= chips // 2 else h - chips) for h in range(1, chips)])
    factors = jnp.concatenate([same, swap(same)])
    turned = pl.pallas_call(
        functools.partial(turn_kernel, rows),
        out_shape=jax.ShapeDtypeStruct((chips * SLICE, 2 * W), jnp.bfloat16),
        in_specs=[HBM],
        out_specs=VMEM,
        scratch_shapes=[pltpu.VMEM((2, W, width), jnp.bfloat16), pltpu.SemaphoreType.DMA((2,))],
        compiler_params=pltpu.CompilerParams(vmem_limit_bytes=50 * MIB),
        cost_estimate=pl.CostEstimate(flops=0, bytes_accessed=2 * MIB, transcendentals=0),
    )(factors)
    arrived, turned = lax.optimization_barrier((arrived, turned))

    own = pl.pallas_call(
        functools.partial(product_kernel, rows, cols),
        out_shape=jax.ShapeDtypeStruct((W, width), jnp.bfloat16),
        in_specs=[HBM, HBM, VMEM, VMEM, HBM],
        out_specs=VMEM,
        scratch_shapes=[
            pltpu.VMEM((W, rows * W), jnp.bfloat16),
            pltpu.VMEM(((rows - 1) * W, width), jnp.bfloat16),
            pltpu.VMEM((W, width), jnp.float32),
            pltpu.SemaphoreType.DMA((rows - 1,)),
            pltpu.SMEM((rows, cols), jnp.int32),
            pltpu.SMEM((cols,), jnp.int32),
            pltpu.SemaphoreType.DMA((2,)),
        ],
        compiler_params=pltpu.CompilerParams(vmem_limit_bytes=50 * MIB),
        cost_estimate=pl.CostEstimate(flops=2 * rows * W * W * width, bytes_accessed=7 * MIB, transcendentals=0),
    )(lists, active_count, arrived, factor, factors)
    other = swap(own)

    def terms(base, dtypes):
        return pl.pallas_call(
            functools.partial(term_kernel, base),
            out_shape=[jax.ShapeDtypeStruct((SLICE, width), dtype) for dtype in dtypes],
            in_specs=[VMEM] * 3,
            out_specs=[VMEM] * len(dtypes),
            compiler_params=pltpu.CompilerParams(vmem_limit_bytes=16 * MIB),
            cost_estimate=pl.CostEstimate(flops=4 * len(dtypes) * SLICE * W * width, bytes_accessed=2 * MIB, transcendentals=0),
        )(turned, own, other)

    def beside(x, way):
        pairs = []
        for i in range(rows):
            pairs.append((i, (i + way * (2 - 4 * (i % 2))) % rows))
        return lax.ppermute(x, "prow", pairs)

    far, near, back, kept = terms(0, [jnp.bfloat16, jnp.bfloat16, jnp.bfloat16, jnp.float32])
    met = [shift(far, 2), beside(near, 1), beside(back, -1)]
    product, base = pl.pallas_call(
        store_kernel,
        out_shape=(jax.ShapeDtypeStruct((W, width), jnp.bfloat16), jax.ShapeDtypeStruct((SLICE, width), jnp.float32)),
        in_specs=[VMEM] * 3,
        out_specs=(HBM, VMEM),
        scratch_shapes=[pltpu.SemaphoreType.DMA],
        compiler_params=pltpu.CompilerParams(vmem_limit_bytes=16 * MIB),
        cost_estimate=pl.CostEstimate(flops=0, bytes_accessed=2 * MIB, transcendentals=0),
    )(own, diag_in[0], kept)
    diagonal = pl.pallas_call(
        sum_kernel,
        out_shape=jax.ShapeDtypeStruct((SLICE, width), jnp.float32),
        in_specs=[VMEM] * chips,
        out_specs=HBM,
        scratch_shapes=[pltpu.VMEM((SLICE, width), jnp.float32), pltpu.SemaphoreType.DMA((4,))],
        compiler_params=pltpu.CompilerParams(vmem_limit_bytes=16 * MIB),
        cost_estimate=pl.CostEstimate(flops=0, bytes_accessed=2 * MIB, transcendentals=0),
    )(base, *met)
    return (product[None, None], diagonal[None])


def solution(mesh):
    placed = (
        P(("pole", "prow"), "pcol"),
        P(("pole", "pcol"), "prow", None, None),
        P(("pole", "pcol"), "prow", None),
        P(),
        P(),
    )
    return jax.shard_map(
        local,
        mesh=mesh,
        in_specs=placed,
        out_specs=(P(("pole", "pcol"), "prow", None, None), P(("pole", "pcol"), "prow", None)),
        check_vma=False,
    )
```
